128 devices in a mesh: grp: 8 (over z, core), dev: 16 (over x, y).
Axes of the slice: x: 4, y: 4, z: 4, core: 2. Of those that a mesh axis runs over, the one named last changes fastest.
Arguments:
- start: float32 [32, 262144], P(None, ('grp', 'dev')), may hold values from -6 to 6
- near_blocks: bfloat16 [20480, 256, 256], P(('grp', 'dev')), may hold values from -0.375 to 0.375
- near_rows: int32 [20480], P(('grp', 'dev')), may hold values from 0 to 127, as said below
- near_cols: int32 [20480], P(('grp', 'dev')), may hold values from 0 to 143, as said below
- near_scale: int32 [20480], P(('grp', 'dev')), may hold values from 0 to 255
- scale_table: float32 [256], replicated, may hold values from 0.05 to 0.5
- near_live: int32 [128], P(('grp', 'dev')), may hold values from 40 to 160, as said below
- leaf_basis: bfloat16 [1024, 64, 256], P(('grp', 'dev')), may hold values from -0.375 to 0.375
- leaf_transfer: float32 [1024, 64, 64], P(('grp', 'dev')), may hold values from -0.25 to 0.25
- device_transfer: float32 [128, 64, 64], P(('grp', 'dev')), may hold values from -0.1875 to 0.1875
- device_coupling: float32 [30, 64, 64], replicated, may hold values from -0.125 to 0.125
- group_coupling: float32 [6, 64, 64], replicated, may hold values from -0.75 to 0.75
Outputs:
- next_basis: float32 [32, 262144], P(None, ('grp', 'dev'))
- hessenberg: float32 [5, 32, 32], replicated
The draws below stay inside these ranges and needn't reach their ends.
Inputs may be any that keep to these rules, and one draw needn't show every extreme that they name: `near_rows`: within each group of 16 devices every cluster of the group is the row of some block slot whose column is the same cluster. `near_cols`: A block's column cluster lies between its row cluster and 16 clusters past it; in the last group it stays below 128. `near_live`: slots below this count are used; in every group one device uses all its slots.
All inputs are finite; a program needn't handle non-finite values.
Results may differ from the reference program's by a relative error of at most 0.0043.
Values may be sent and summed in bfloat16 or wider, within the bound.
A program may use at most 128 MiB of HBM per device.

```python
import math
import jax
import jax.numpy as jnp
from jax import lax

P_SIZE = 256
R = 32
K = 64
CL_DEV = 8
NSCALE = 256
REACH = 16
NB_DEV = 160
CL_GRP = 128
CLUSTERS = 1024
NPAN = 262144
NB_ALL = 20480
DOFF = 30
GOFF = 6
N_GRP = 8
N_DEV = 16
DEVICES = 128


def near_lists(key):
    per_group = N_DEV * NB_DEV
    key_center, key_first, key_second, key_offset, key_order = jax.random.split(key, 5)
    slot = jnp.arange(per_group, dtype=jnp.int32)[None, :]
    center = jax.random.randint(key_center, (N_GRP, 1), 0, CL_GRP, dtype=jnp.int32)
    first = jax.random.randint(key_first, (N_GRP, per_group), 0, CL_GRP, dtype=jnp.int32)
    second = jax.random.randint(key_second, (N_GRP, per_group), 0, CL_GRP, dtype=jnp.int32)
    extra = (center + jnp.minimum(first, second)) % CL_GRP
    row_ids = jnp.where(slot < CL_GRP, slot, extra)
    row_ids = jnp.where(slot == CL_GRP, CL_GRP - 1, row_ids)
    offset = jax.random.randint(key_offset, (N_GRP, per_group), 0, REACH + 1, dtype=jnp.int32)
    offset = jnp.where(slot < CL_GRP, 0, offset)
    offset = jnp.where(slot == CL_GRP, REACH, offset)
    column_ids = row_ids + offset
    last_group = jnp.arange(N_GRP, dtype=jnp.int32)[:, None] == N_GRP - 1
    column_ids = jnp.where(last_group, jnp.minimum(column_ids, CL_GRP - 1), column_ids)
    scores = jax.random.randint(key_order, (N_GRP, per_group), 0, 4096, dtype=jnp.int32) * per_group + slot
    order = jnp.argsort(scores, axis=1)
    row_ids = jnp.take_along_axis(row_ids, order, axis=1).reshape(-1)
    column_ids = jnp.take_along_axis(column_ids, order, axis=1).reshape(-1)
    return (row_ids.astype(jnp.int32), column_ids.astype(jnp.int32))


def draw_near_rows(key, part):
    return near_lists(key)[0]


def draw_near_cols(key, part):
    return near_lists(key)[1]


def draw_near_live(key, part):
    key = jax.random.fold_in(key, 7)
    key_count, key_busy = jax.random.split(key, 2)
    counts = jax.random.randint(key_count, (N_GRP, N_DEV), NB_DEV // 4, 3 * NB_DEV // 4 + 1, dtype=jnp.int32)
    busy = jax.random.randint(key_busy, (N_GRP, 1), 0, N_DEV, dtype=jnp.int32)
    places = jnp.arange(N_DEV, dtype=jnp.int32)[None, :]
    counts = jnp.where(places == busy, NB_DEV, counts)
    counts = jnp.where(places == (busy + 1) % N_DEV, NB_DEV // 4, counts)
    return counts.reshape(-1).astype(jnp.int32)


def plant(values, stream_key, least, top_value):
    longest = values.shape.index(max(values.shape))
    spots = []
    for shift in (0, 1):
        where = [jax.random.randint(jax.random.fold_in(stream_key, axis), (), 0, length) for axis, length in enumerate(values.shape)]
        where[longest] = (where[longest] + shift) % values.shape[longest]
        spots.append(tuple(where))
    return values.at[spots[0]].set(least).at[spots[1]].set(top_value)


def shard_levels(stream_key, shape, cuts, least, high):
    def one(position, blocks):
        steps = jax.random.uniform(jax.random.fold_in(jax.random.fold_in(stream_key, 6), position), (blocks,), jnp.float32, least / len(cuts), high / len(cuts))
        return jnp.repeat(jnp.exp(steps), shape[position] // blocks).reshape((-1,) + (1,) * (len(shape) - position - 1))

    loudness = one(*cuts[0])
    for cut in cuts[1:]:
        loudness = loudness * one(*cut)
    return loudness


def gaussian(rng, shape, spread, reach, shards=(), held_as=jnp.bfloat16):
    loudness = shard_levels(rng, shape, shards, -0.22, 0.18) if shards else 1.0
    entries = jax.random.normal(rng, shape, jnp.float32) * spread * loudness
    return jnp.minimum(jnp.maximum(entries, -reach), reach).astype(held_as)


def setup_inputs(seed: int = 0) -> dict:
    streams_of = jax.random.split(jax.random.key(seed), 13)
    return {
        "start": gaussian(streams_of[0], (R, NPAN), 1.0, 6.0, ((1, 128),), jnp.float32),
        "near_blocks": gaussian(streams_of[1], (NB_ALL, P_SIZE, P_SIZE), P_SIZE ** -0.5, 0.375, ((0, 128),)),
        "near_rows": draw_near_rows(jax.random.fold_in(streams_of[12], 71), 0),
        "near_cols": draw_near_cols(jax.random.fold_in(streams_of[12], 71), 0),
        "near_scale": plant(jax.random.randint(streams_of[4], (NB_ALL,), 0, NSCALE), jax.random.fold_in(streams_of[4], 1), 0, NSCALE - 1).astype(jnp.int32),
        "scale_table": jnp.clip(jnp.exp(jax.random.uniform(streams_of[5], (NSCALE,), jnp.float32, math.log(0.05), math.log(0.5))), 0.05, 0.5),
        "near_live": draw_near_live(jax.random.fold_in(streams_of[12], 71), 0),
        "leaf_basis": gaussian(streams_of[7], (CLUSTERS, K, P_SIZE), P_SIZE ** -0.5, 0.375, ((0, 128),)),
        "leaf_transfer": gaussian(streams_of[8], (CLUSTERS, K, K), (K * CL_DEV) ** -0.5, 0.25, ((0, 128),), jnp.float32),
        "device_transfer": gaussian(streams_of[9], (DEVICES, K, K), (K * N_DEV) ** -0.5, 0.1875, ((0, 128),), jnp.float32),
        "device_coupling": gaussian(streams_of[10], (DOFF, K, K), (2 * K * N_DEV) ** -0.5, 0.125, (), jnp.float32),
        "group_coupling": gaussian(streams_of[11], (GOFF, K, K), K ** -0.5, 0.75, (), jnp.float32),
    }


def shifted(table, offset):
    count = table.shape[0]
    zero_rows = jnp.zeros((abs(offset),) + table.shape[1:], jnp.float32)
    if offset > 0:
        return jnp.concatenate([table[offset:], zero_rows], axis=0)
    return jnp.concatenate([zero_rows, table[:count + offset]], axis=0)

def reference(start, near_blocks, near_rows, near_cols, near_scale, scale_table, near_live, leaf_basis, leaf_transfer, device_transfer, device_coupling, group_coupling):
    highest = lax.Precision.HIGHEST
    slot_ids = jnp.arange(NB_DEV, dtype=jnp.int32)
    device_ids = jnp.arange(DEVICES, dtype=jnp.int32)
    group_of = device_ids // N_DEV
    weights = scale_table[near_scale].reshape(DEVICES, NB_DEV) * (slot_ids[None, :] < near_live[:, None]).astype(jnp.float32)
    first_cluster = (group_of * CL_GRP)[:, None]
    row_list = (near_rows.reshape(DEVICES, NB_DEV) + first_cluster).astype(jnp.int32)
    column_list = (near_cols.reshape(DEVICES, NB_DEV) + first_cluster).astype(jnp.int32)
    device_blocks = near_blocks.reshape(DEVICES, NB_DEV, P_SIZE, P_SIZE)

    def near_apply(panels):

        def visit_device(accumulated, device_item):
            pair_blocks, row_ids, column_ids, pair_weights = device_item
            pair_blocks = pair_blocks.astype(jnp.float32)
            to_rows = jnp.einsum('kij,rkj->rki', pair_blocks, panels[:, column_ids], precision=highest) * pair_weights[None, :, None]
            to_columns = jnp.einsum('kij,rki->rkj', pair_blocks, panels[:, row_ids], precision=highest) * pair_weights[None, :, None]
            accumulated = accumulated.at[:, row_ids].add(to_rows).at[:, column_ids].add(to_columns)
            return (accumulated, None)
        accumulated, unused = lax.scan(visit_device, jnp.zeros((R, CLUSTERS, P_SIZE), jnp.float32), (device_blocks, row_list, column_list, weights))
        return accumulated

    def far_apply(panels):
        basis_wide = leaf_basis.astype(jnp.float32)
        leaf_coeffs = jnp.einsum('ckp,rcp->ckr', basis_wide, panels, precision=highest)
        lifted = jnp.einsum('cjk,ckr->cjr', leaf_transfer, leaf_coeffs, precision=highest)
        device_coeffs = jnp.sum(lifted.reshape(DEVICES, CL_DEV, K, R), axis=1)
        parents = jnp.einsum('djk,dkr->djr', device_transfer, device_coeffs, precision=highest)
        group_coeffs = jnp.sum(parents.reshape(N_GRP, N_DEV, K, R), axis=1)
        field = jnp.zeros((DEVICES, K, R), jnp.float32)
        for offset in range(2, 2 * N_DEV):
            coupling = device_coupling[offset - 2]
            ahead_valid = (device_ids + offset < DEVICES) & ((device_ids + offset) // N_DEV - group_of <= 1)
            behind_valid = (device_ids - offset >= 0) & (group_of - (device_ids - offset) // N_DEV <= 1)
            ahead = jnp.einsum('jk,dkr->djr', coupling, shifted(device_coeffs, offset), precision=highest)
            behind = jnp.einsum('kj,dkr->djr', coupling, shifted(device_coeffs, -offset), precision=highest)
            field = field + jnp.where(ahead_valid[:, None, None], ahead, 0.0) + jnp.where(behind_valid[:, None, None], behind, 0.0)
        top_field = jnp.zeros((N_GRP, K, R), jnp.float32)
        for offset in range(2, N_GRP):
            coupling = group_coupling[offset - 2]
            top_field = top_field + jnp.einsum('jk,gkr->gjr', coupling, shifted(group_coeffs, offset), precision=highest)
            top_field = top_field + jnp.einsum('kj,gkr->gjr', coupling, shifted(group_coeffs, -offset), precision=highest)
        field = field + jnp.einsum('dkj,dkr->djr', device_transfer, jnp.repeat(top_field, N_DEV, axis=0), precision=highest)
        leaf_fields = jnp.einsum('ckj,ckr->cjr', leaf_transfer, jnp.repeat(field, CL_DEV, axis=0), precision=highest)
        return jnp.einsum('ckp,ckr->rcp', basis_wide, leaf_fields, precision=highest)

    def operate(values):
        rounded = lax.optimization_barrier(values.astype(jnp.bfloat16))
        panels = rounded.astype(jnp.float32).reshape(R, CLUSTERS, P_SIZE)
        return 0.5 * values + (near_apply(panels) + far_apply(panels)).reshape(R, NPAN)

    def inner_product(left, right):
        return jnp.dot(left, right.T, precision=highest) / NPAN

    def orthonormal(panel_block):
        factor = jnp.linalg.cholesky(inner_product(panel_block, panel_block))
        return (lax.linalg.triangular_solve(factor, panel_block, left_side=True, lower=True), factor)
    basis_one, start_factor = orthonormal(start)
    product_one = operate(basis_one)
    hess_a = inner_product(basis_one, product_one)
    remainder_one = product_one - jnp.dot(hess_a.T, basis_one, precision=highest)
    basis_two, factor_one = orthonormal(remainder_one)
    product_two = operate(basis_two)
    hess_b = inner_product(basis_one, product_two)
    hess_c = inner_product(basis_two, product_two)
    remainder_two = product_two - jnp.dot(hess_b.T, basis_one, precision=highest) - jnp.dot(hess_c.T, basis_two, precision=highest)
    next_basis, factor_two = orthonormal(remainder_two)
    return (next_basis, jnp.stack([hess_a, factor_one, hess_b, hess_c, factor_two]))
```

```python
import functools

import jax
import jax.numpy as jnp
from jax import lax
from jax.experimental import pallas as pl
from jax.experimental.pallas import tpu as pltpu
from jax.sharding import PartitionSpec as P

F32 = jnp.float32
BF16 = jnp.bfloat16
HIGHEST = lax.Precision.HIGHEST
MESH = pl.DeviceIdType.MESH

R = 32
K = 64
HALF = 128
ND = 16
NG = 8
CL = 8
NB = 160
NCL = ND * CL
WIN = NCL + 16
NOFF = 30
GOFF = 6
UNROLL = 16
NPAN = 262144

NN = (((1,), (0,)), ((), ()))
NT = (((1,), (1,)), ((), ()))


def dot(a, b, dims=NN):
    return lax.dot_general(a, b, dims, precision=HIGHEST, preferred_element_type=F32)


def bdot(a, b, dims=NN):
    return lax.dot_general(a, b, dims, preferred_element_type=F32)


def split(v):
    hi = v.astype(BF16)
    return hi, (v - hi.astype(F32)).astype(BF16)


def pack(v):
    return jnp.concatenate([v[0:8], v[8:16], v[16:24], v[24:32]], axis=1)


def unpack(v):
    return jnp.concatenate([v[:, 0:32], v[:, 32:64], v[:, 64:96], v[:, 96:128]], axis=0)


def factor(gram):
    row = lax.broadcasted_iota(jnp.int32, (R, R), 0)
    col = lax.broadcasted_iota(jnp.int32, (R, R), 1)
    eye = (row == col).astype(F32)
    rid = lax.broadcasted_iota(jnp.int32, (R, 1), 0)
    m = jnp.concatenate([gram, eye], axis=1)
    for k in range(R - 1):
        pivot = m[k : k + 1, :]
        inverse = 1.0 / m[k : k + 1, k : k + 1]
        scale = jnp.where(rid > k, m[:, k : k + 1] * inverse, 0.0)
        m = m - scale * pivot
    upper = m[:, :R]
    diag = jnp.sum(jnp.where(row == col, upper, 0.0), axis=1, keepdims=True)
    rs = 1.0 / jnp.sqrt(diag)
    lower = jnp.where(row <= col, upper * rs, 0.0).T
    return lower, jnp.where(row >= col, m[:, R:] * rs, 0.0)


def permuted(c):
    return jnp.where(c < NCL, ((c >> 3) & 3) * 32 + (c >> 5) * 8 + (c & 7), c)


NAMES = [
    "p1p", "p1m", "q0p", "q0m", "f1p", "f1m", "q1p", "q1m", "q2p", "q2m", "q3p", "q3m", "g0", "g1", "g2", "g3",
    "z0", "z1", "ov", "s1p", "s1m", "s2p", "s2m", "s3p", "s3m", "t1p", "t1m", "t2p", "t2m", "t3p", "t3m",
]
NUMBER = {(n, h): 2 * i + h for i, n in enumerate(NAMES) for h in range(2)}
QUP = 2 * len(NAMES)
QDN = QUP + 1
SEM_AR1 = QDN + 1
SEM_AR2 = SEM_AR1 + ND
SEM_FAR1 = SEM_AR2 + NG
SEM_FAR2 = SEM_FAR1 + ND
NSEM = SEM_FAR2 + NG


def kernel(
    rows, cols, scl, table, live, prev, last,
    start, lbasis, ltrans, dtrans, dcoup, gcoup, blocks_hbm,
    next_ref, hess_ref,
    blocks, seg, w0, w1, t0, t1, over, xbuf, ybuf, sbuf, ubuf, vbuf, mbuf, gbuf, ar1, ar2,
    ltcat, cah, cal, cbh, cbl, dah, dal, dbh, dbl, b1, b2, u, bsem, ssem, rsem,
):
    g = lax.axis_index("grp")
    d = lax.axis_index("dev")
    x, y = d // 4, d % 4
    w = (w0, w1)
    t = (t0, t1)
    ab = ((x, y), (y, x))

    def dev(h, a, b):
        return a * 4 + b if h == 0 else b * 4 + a

    def step(v, k):
        return (v + k) % 4

    near_copy = pltpu.make_async_copy(blocks_hbm, blocks, bsem.at[0])
    near_copy.start()

    def remote(src, dst, number, gg, dd):
        return pltpu.make_async_remote_copy(
            src_ref=src, dst_ref=dst, send_sem=ssem.at[number], recv_sem=rsem.at[number],
            device_id=(gg, dd), device_id_type=MESH,
        )

    mbuf[...] = jnp.zeros_like(mbuf)
    gbuf[...] = jnp.zeros_like(gbuf)
    over[...] = jnp.zeros_like(over)
    for h in range(2):
        w[h][NCL:WIN] = jnp.zeros((16, R, HALF), BF16)
    seg[2 * NB] = jnp.zeros((R, 2 * HALF), F32)

    barrier = pltpu.get_barrier_semaphore()

    def greet_dev(o, c):
        pl.semaphore_signal(barrier, inc=1, device_id=(g, (d + o) % ND), device_id_type=MESH)
        return c

    def greet_grp(o, c):
        pl.semaphore_signal(barrier, inc=1, device_id=((g + o) % NG, d), device_id_type=MESH)
        return c

    lax.fori_loop(1, ND, greet_dev, 0)
    lax.fori_loop(1, NG, greet_grp, 0)

    def all_reduce(i, parts, beside=None, first=False):
        n = 8 * len(parts)
        val = jnp.concatenate([pack(p) for p in parts], axis=0) if len(parts) > 1 else pack(parts[0])
        ar1[i, d, 0:n] = val
        if first:
            pl.semaphore_wait(barrier, ND + NG - 2)

        def along_dev(o):
            return remote(ar1.at[i, d, pl.ds(0, n)], ar1.at[i, d, pl.ds(0, n)], SEM_AR1 + o, g, (d + o) % ND)

        def along_grp(o):
            return remote(ar2.at[i, g, pl.ds(0, n)], ar2.at[i, g, pl.ds(0, n)], SEM_AR2 + o, (g + o) % NG, d)

        def go(make, count):
            lax.fori_loop(1, count, lambda o, c: (make(o).start(), c)[1], 0)

        def got(make, count):
            lax.fori_loop(1, count, lambda o, c: (make(o).wait_recv(), c)[1], 0)

        def left(make, count):
            lax.fori_loop(1, count, lambda o, c: (make(o).wait_send(), c)[1], 0)

        go(along_dev, ND)
        if beside is not None:
            beside()
        got(along_dev, ND)
        total = ar1[i, 0, 0:n]
        for e in range(1, ND):
            total = total + ar1[i, e, 0:n]
        ar2[i, g, 0:n] = total
        go(along_grp, NG)
        left(along_dev, ND)
        got(along_grp, NG)
        total = ar2[i, 0, 0:n]
        for e in range(1, NG):
            total = total + ar2[i, e, 0:n]
        left(along_grp, NG)
        total = total * (1.0 / NPAN)
        return [unpack(total[8 * j : 8 * j + 8]) for j in range(len(parts))]

    def tables():
        for i in range(CL // 2):
            ltcat[:, 128 * i : 128 * i + 128] = jnp.concatenate([ltrans[2 * i], ltrans[2 * i + 1]], axis=1)

        def build(src, count, ah, al, bh, bl):
            for i in range(count // 2):
                at = slice(128 * i, 128 * i + 128)
                ahead = jnp.concatenate([src[2 * i], src[2 * i + 1]], axis=1)
                ah[:, at], al[:, at] = split(ahead)
                o = count - 1 - 2 * i
                behind = jnp.concatenate([src[o], src[o - 1]], axis=0).T
                bh[:, at], bl[:, at] = split(behind)

        build(dcoup, NOFF, cah, cal, cbh, cbl)
        build(gcoup, GOFF, dah, dal, dbh, dbl)

    def far_send(i):
        return remote(
            mbuf.at[pl.ds((32 + d) * K, K)], mbuf.at[pl.ds((32 + d) * K, K)], SEM_FAR1 + i, g, (d + i) % ND
        )

    def top_send(i):
        return remote(gbuf.at[pl.ds((8 + g) * K, K)], gbuf.at[pl.ds((8 + g) * K, K)], SEM_FAR2 + i, (g + i) % NG, d)

    def apply(v_ref):
        vb = v_ref[...].astype(BF16)
        for h in range(2):
            for c in range(CL):
                lo = c * 256 + h * HALF
                w[h][(ab[h][0] * 4 + ab[h][1]) * CL + c] = vb[:, lo : lo + HALF]

        def ship(name, h, src, dst, dd, gg=None):
            c = remote(src, dst, NUMBER[name, h], g if gg is None else gg, dd)
            c.start()
            return c

        sent = []

        def shard(h, a, b, lo=0, n=CL):
            return w[h].at[pl.ds((a * 4 + b) * CL + lo, n)]

        def same(name, h, ref, dd):
            c = ship(name, h, ref, ref, dd)
            sent.append(c)
            return c

        cp = {}
        for h in range(2):
            a, b = ab[h]
            own = shard(h, a, b)
            cp["p1p", h] = same("p1p", h, own, dev(h, a, step(b, 1)))
            cp["p1m", h] = same("p1m", h, own, dev(h, a, step(b, 3)))
            cp["q0p", h] = same("q0p", h, own, dev(h, step(a, 1), b))
            cp["q0m", h] = same("q0m", h, own, dev(h, step(a, 3), b))

        q = jnp.concatenate([bdot(lbasis[c], vb[:, 256 * c : 256 * c + 256], NT) for c in range(CL)], axis=0)
        coeffs = dot(ltcat[...], q)
        parents = dot(dtrans[0], coeffs)
        qh, ql = split(coeffs)
        ph, pe = split(parents)
        mbuf[pl.ds(pl.multiple_of((32 + d) * K, K), K), :] = jnp.concatenate([qh, ql, ph, pe], axis=1)
        lax.fori_loop(1, ND, lambda o, c: (far_send(o).start(), c)[1], 0)

        for h in range(2):
            a, b = ab[h]
            cp["p1p", h].wait_recv()
            back = shard(h, a, step(b, 3))
            cp["f1p", h] = same("f1p", h, shard(h, a, step(b, 3), 0, 4), dev(h, a, step(b, 1)))
            cp["q1p", h] = same("q1p", h, back, dev(h, step(a, 1), b))
            cp["q1m", h] = same("q1m", h, back, dev(h, step(a, 3), b))
            cp["p1m", h].wait_recv()
            ahead = shard(h, a, step(b, 1))
            cp["f1m", h] = same("f1m", h, shard(h, a, step(b, 1), 4, 4), dev(h, a, step(b, 3)))
            cp["q2p", h] = same("q2p", h, ahead, dev(h, step(a, 1), b))
            cp["q2m", h] = same("q2m", h, ahead, dev(h, step(a, 3), b))
        for h in range(2):
            a, b = ab[h]
            cp["q0p", h].wait_recv()
            cp["g0", h] = same("g0", h, shard(h, step(a, 3), b), dev(h, step(a, 1), b))
            cp["q0m", h].wait_recv()
        for h in range(2):
            a, b = ab[h]
            cp["f1p", h].wait_recv()
            cp["f1m", h].wait_recv()
            across = shard(h, a, step(b, 2))
            cp["q3p", h] = same("q3p", h, across, dev(h, step(a, 1), b))
            cp["q3m", h] = same("q3m", h, across, dev(h, step(a, 3), b))

        lax.fori_loop(1, ND, lambda o, c: (far_send(o).wait_recv(), c)[1], 0)
        group_rows = pl.ds(32 * K, ND * K)
        up = remote(mbuf.at[group_rows], mbuf.at[pl.ds(16 * K, ND * K)], QUP, (g + 1) % NG, d)
        down = remote(mbuf.at[group_rows], mbuf.at[pl.ds(48 * K, ND * K)], QDN, (g + NG - 1) % NG, d)

        @pl.when(g < NG - 1)
        def _():
            up.start()

        @pl.when(g > 0)
        def _():
            down.start()

        top = mbuf[32 * K : 33 * K, :].astype(F32)
        for e in range(1, ND):
            top = top + mbuf[(32 + e) * K : (33 + e) * K, :].astype(F32)
        gh, gl = split(top[:, 64:96] + top[:, 96:128])
        gbuf[pl.ds(pl.multiple_of((8 + g) * K, K), K), :] = jnp.concatenate(
            [gh, gl, jnp.zeros((K, 64), BF16)], axis=1
        )
        lax.fori_loop(1, NG, lambda o, c: (top_send(o).start(), c)[1], 0)

        for h in range(2):
            a, b = ab[h]
            cp["q1p", h].wait_recv()
            cp["g1", h] = same("g1", h, shard(h, step(a, 3), step(b, 3)), dev(h, step(a, 1), b))
            cp["q1m", h].wait_recv()
            cp["q2m", h].wait_recv()
            cp["g2", h] = same("g2", h, shard(h, step(a, 1), step(b, 1)), dev(h, step(a, 3), b))
            cp["q2p", h].wait_recv()
        for h in range(2):
            a, b = ab[h]
            cp["q3m", h].wait_recv()
            cp["g3", h] = same("g3", h, shard(h, step(a, 1), step(b, 2)), dev(h, step(a, 3), b))
            cp["q3p", h].wait_recv()

        lax.fori_loop(1, NG, lambda o, c: (top_send(o).wait_recv(), c)[1], 0)

        @pl.when(g > 0)
        def _():
            up.wait_recv()

        @pl.when(g < NG - 1)
        def _():
            down.wait_recv()

        ga = gbuf[pl.ds(pl.multiple_of((10 + g) * K, K), GOFF * K), :]
        gb = gbuf[pl.ds(pl.multiple_of((1 + g) * K, K), GOFF * K), :]
        s1 = bdot(dah[...], ga) + bdot(dbh[...], gb)
        s2 = bdot(dal[...], ga) + bdot(dbl[...], gb)
        top_field = s1[:, 0:32] + s1[:, 32:64] + s2[:, 0:32]
        qa = mbuf[pl.ds(pl.multiple_of((34 + d) * K, K), NOFF * K), :]
        qb = mbuf[pl.ds(pl.multiple_of((1 + d) * K, K), NOFF * K), :]
        s1 = bdot(cah[...], qa) + bdot(cbh[...], qb)
        s2 = bdot(cal[...], qa) + bdot(cbl[...], qb)
        field = s1[:, 0:32] + s1[:, 32:64] + s2[:, 0:32]
        field_t = field.T + dot(top_field.T, dtrans[0])
        leaf_t = dot(field_t, ltcat[...])
        lh, ll = split(leaf_t)
        for c in range(CL):
            both = jnp.concatenate([lh[:, K * c : K * c + K], ll[:, K * c : K * c + K]], axis=0)
            far = bdot(both, lbasis[c])
            u[:, 256 * c : 256 * c + 256] = far[:R] + far[R:]

        for h in range(2):
            for n in ("g0", "g1", "g2", "g3"):
                cp[n, h].wait_recv()

        for h in range(2):
            for s in range(2):
                at = 4 if (h, s) == (1, 1) else s
                cp["z%d" % s, h] = remote(
                    w[h].at[pl.ds(at * CL, CL)], w[h].at[pl.ds(NCL + s * CL, CL)], NUMBER["z%d" % s, h], (g + NG - 1) % NG, d
                )

        @pl.when(g > 0)
        def _():
            for h in range(2):
                for s in range(2):
                    cp["z%d" % s, h].start()

        lax.fori_loop(1, ND, lambda o, c: (far_send(o).wait_send(), c)[1], 0)
        lax.fori_loop(1, NG, lambda o, c: (top_send(o).wait_send(), c)[1], 0)
        for c in sent:
            c.wait_send()

        @pl.when(g < NG - 1)
        def _():
            up.wait_send()
            for h in range(2):
                for s in range(2):
                    cp["z%d" % s, h].wait_recv()

        @pl.when(g > 0)
        def _():
            down.wait_send()

        n_live = live[0]

        def near(i, carry):
            for j in range(UNROLL):
                k = i * UNROLL + j
                r, c = rows[k], cols[k]
                weight = jnp.where(k < n_live, table[scl[k]], 0.0)
                block = blocks[k]
                vc = jnp.concatenate([w0[c], w1[permuted(c)]], axis=1)
                vr = jnp.concatenate([w0[r], w1[permuted(r)]], axis=1)
                to_row = bdot(block, vc, NT).T
                to_col = bdot(vr, block)
                seg[2 * k] = seg[prev[2 * k]] + weight * to_row
                seg[2 * k + 1] = seg[prev[2 * k + 1]] + weight * to_col
            return carry

        lax.fori_loop(0, NB // UNROLL, near, 0)

        @pl.when(g > 0)
        def _():
            for h in range(2):
                for s in range(2):
                    cp["z%d" % s, h].wait_send()

        for c in range(NCL, WIN):
            v = seg[last[c]]
            t0[c] = v[:, :HALF].astype(BF16)
            t1[c] = v[:, HALF:].astype(BF16)
        ov = [remote(t[h].at[pl.ds(NCL, 16)], over.at[h], NUMBER["ov", h], (g + 1) % NG, d) for h in range(2)]

        @pl.when(g < NG - 1)
        def _():
            for c in ov:
                c.start()

        def totals(i, carry):
            for j in range(CL):
                v = seg[last[i * CL + j]]
                t0[i * CL + j] = v[:, :HALF].astype(BF16)
                t1[(i % 4) * 32 + (i // 4) * CL + j] = v[:, HALF:].astype(BF16)
            return carry

        lax.fori_loop(2, ND, totals, 0)

        @pl.when(g > 0)
        def _():
            for c in ov:
                c.wait_recv()

        for i in range(2):
            for j in range(CL):
                v = seg[last[i * CL + j]]
                t0[i * CL + j] = (v[:, :HALF] + over[0, i * CL + j].astype(F32)).astype(BF16)
                t1[i * 32 + j] = (v[:, HALF:] + over[1, i * CL + j].astype(F32)).astype(BF16)

        sent.clear()

        def piece(h, a, lo):
            return t[h].at[pl.ds(a * 32 + lo, 16)]

        def to(name, h, src, dst, dd):
            cp[name, h] = ship(name, h, src, dst, dd)
            sent.append(cp[name, h])

        for h in range(2):
            a, b = ab[h]
            fwd, bwd = dev(h, step(a, 1), b), dev(h, step(a, 3), b)
            to("s1p", h, piece(h, step(a, 2), 0), xbuf.at[h, 0], fwd)
            to("s1m", h, piece(h, step(a, 2), 16), xbuf.at[h, 1], bwd)
            to("s2p", h, piece(h, step(a, 1), 16), ybuf.at[h, 0, pl.ds(16, 16)], fwd)
            to("s2m", h, piece(h, step(a, 3), 0), ybuf.at[h, 1, pl.ds(0, 16)], bwd)
        for h in range(2):
            a, b = ab[h]
            fwd, bwd = dev(h, step(a, 1), b), dev(h, step(a, 3), b)
            cp["s1p", h].wait_recv()
            at = pl.ds(step(a, 1) * 32, 16)
            t[h][at] = (t[h][at].astype(F32) + xbuf[h, 0].astype(F32)).astype(BF16)
            to("s3p", h, piece(h, step(a, 1), 0), ybuf.at[h, 0, pl.ds(0, 16)], fwd)
            cp["s1m", h].wait_recv()
            at = pl.ds(step(a, 3) * 32 + 16, 16)
            t[h][at] = (t[h][at].astype(F32) + xbuf[h, 1].astype(F32)).astype(BF16)
            to("s3m", h, piece(h, step(a, 3), 16), ybuf.at[h, 1, pl.ds(16, 16)], bwd)
        for h in range(2):
            a, b = ab[h]
            fwd, bwd = dev(h, a, step(b, 1)), dev(h, a, step(b, 3))
            for n in ("s2p", "s2m", "s3p", "s3m"):
                cp[n, h].wait_recv()
            for j in range(4):
                at = pl.ds(j * CL, CL)
                mine = t[h][pl.ds(a * 32 + j * CL, CL)].astype(F32)
                sbuf[h, at] = mine + ybuf[h, 0, at].astype(F32) + ybuf[h, 1, at].astype(F32)

            def part(k, lo):
                return sbuf.at[h, pl.ds(step(b, k) * CL + lo, 4)]

            to("t1p", h, part(2, 0), ubuf.at[h, 0], fwd)
            to("t1m", h, part(2, 4), ubuf.at[h, 1], bwd)
            to("t2p", h, part(1, 4), vbuf.at[h, 0, pl.ds(4, 4)], fwd)
            to("t2m", h, part(3, 0), vbuf.at[h, 1, pl.ds(0, 4)], bwd)
        for h in range(2):
            a, b = ab[h]
            fwd, bwd = dev(h, a, step(b, 1)), dev(h, a, step(b, 3))
            cp["t1p", h].wait_recv()
            at = pl.ds(step(b, 1) * CL, 4)
            sbuf[h, at] = sbuf[h, at] + ubuf[h, 0]
            to("t3p", h, sbuf.at[h, at], vbuf.at[h, 0, pl.ds(0, 4)], fwd)
            cp["t1m", h].wait_recv()
            at = pl.ds(step(b, 3) * CL + 4, 4)
            sbuf[h, at] = sbuf[h, at] + ubuf[h, 1]
            to("t3m", h, sbuf.at[h, at], vbuf.at[h, 1, pl.ds(4, 4)], bwd)
        for h in range(2):
            a, b = ab[h]
            for n in ("t2p", "t2m", "t3p", "t3m"):
                cp[n, h].wait_recv()
            for c in range(CL):
                total = sbuf[h, b * CL + c] + vbuf[h, 0, c] + vbuf[h, 1, c]
                lo = 256 * c + h * HALF
                u[:, lo : lo + HALF] = u[:, lo : lo + HALF] + total
        for c in sent:
            c.wait_send()

        @pl.when(g < NG - 1)
        def _():
            for c in ov:
                c.wait_send()

    row = lax.broadcasted_iota(jnp.int32, (R, R), 0)
    col = lax.broadcasted_iota(jnp.int32, (R, R), 1)
    half_eye = jnp.where(row == col, 0.5, 0.0)

    s = start[...]
    (gram,) = all_reduce(0, [dot(s, s, NT)], beside=tables, first=True)
    _, inverse = factor(gram)
    b1[...] = dot(inverse, s)
    near_copy.wait()
    apply(b1)

    uu = u[...]
    ha, gram = all_reduce(1, [dot(b1[...], uu, NT), dot(uu, uu, NT)])
    lower1, inverse = factor(gram - lax.dot_general(ha, ha, (((0,), (0,)), ((), ())), precision=HIGHEST))
    b2[...] = dot(inverse, uu) - dot(dot(inverse, ha, NT), b1[...])
    hess_ref[0] = ha + half_eye
    hess_ref[1] = lower1
    apply(b2)

    uu = u[...]
    hb, hc, gram = all_reduce(2, [dot(b1[...], uu, NT), dot(b2[...], uu, NT), dot(uu, uu, NT)])
    tn = (((0,), (0,)), ((), ()))
    gram = gram - dot(hb, hb, tn) - dot(hc, hc, tn)
    lower2, inverse = factor(gram)
    next_ref[...] = dot(inverse, uu) - dot(dot(inverse, hb, NT), b1[...]) - dot(dot(inverse, hc, NT), b2[...])
    hess_ref[2] = hb
    hess_ref[3] = hc + half_eye
    hess_ref[4] = lower2


def chains(near_rows, near_cols):
    target = jnp.stack([near_rows, near_cols], axis=1).reshape(-1)
    order = jnp.arange(2 * NB, dtype=jnp.int32)
    before = (target[:, None] == target[None, :]) & (order[None, :] < order[:, None])
    prev = jnp.max(jnp.where(before, order[None, :], -1), axis=1)
    hit = jnp.arange(WIN, dtype=jnp.int32)[:, None] == target[None, :]
    last = jnp.max(jnp.where(hit, order[None, :], -1), axis=1)
    return jnp.where(prev < 0, 2 * NB, prev), jnp.where(last < 0, 2 * NB, last)


def shards(
    start, near_blocks, near_rows, near_cols, near_scale, scale_table, near_live,
    leaf_basis, leaf_transfer, device_transfer, device_coupling, group_coupling,
):
    prev, last = chains(near_rows, near_cols)
    smem = pl.BlockSpec(memory_space=pltpu.SMEM)
    vmem = pl.BlockSpec(memory_space=pltpu.VMEM)
    return pl.pallas_call(
        kernel,
        out_shape=(jax.ShapeDtypeStruct((R, 2048), F32), jax.ShapeDtypeStruct((5, R, R), F32)),
        in_specs=[smem] * 7 + [vmem] * 6 + [pl.BlockSpec(memory_space=pl.ANY)],
        out_specs=(vmem, vmem),
        scratch_shapes=[
            pltpu.VMEM((NB, 256, 256), BF16),
            pltpu.VMEM((2 * NB + 1, R, 256), F32),
            pltpu.VMEM((WIN, R, HALF), BF16),
            pltpu.VMEM((WIN, R, HALF), BF16),
            pltpu.VMEM((WIN, R, HALF), BF16),
            pltpu.VMEM((WIN, R, HALF), BF16),
            pltpu.VMEM((2, 16, R, HALF), BF16),
            pltpu.VMEM((2, 2, 16, R, HALF), BF16),
            pltpu.VMEM((2, 2, 32, R, HALF), BF16),
            pltpu.VMEM((2, 32, R, HALF), F32),
            pltpu.VMEM((2, 2, 4, R, HALF), F32),
            pltpu.VMEM((2, 2, 8, R, HALF), F32),
            pltpu.VMEM((80 * K, 128), BF16),
            pltpu.VMEM((24 * K, 128), BF16),
            pltpu.VMEM((3, ND, 24, 128), F32),
            pltpu.VMEM((3, NG, 24, 128), F32),
            pltpu.VMEM((K, CL * K), F32),
            pltpu.VMEM((K, NOFF * K), BF16),
            pltpu.VMEM((K, NOFF * K), BF16),
            pltpu.VMEM((K, NOFF * K), BF16),
            pltpu.VMEM((K, NOFF * K), BF16),
            pltpu.VMEM((K, GOFF * K), BF16),
            pltpu.VMEM((K, GOFF * K), BF16),
            pltpu.VMEM((K, GOFF * K), BF16),
            pltpu.VMEM((K, GOFF * K), BF16),
            pltpu.VMEM((R, 2048), F32),
            pltpu.VMEM((R, 2048), F32),
            pltpu.VMEM((R, 2048), F32),
            pltpu.SemaphoreType.DMA((1,)),
            pltpu.SemaphoreType.DMA((NSEM,)),
            pltpu.SemaphoreType.DMA((NSEM,)),
        ],
        compiler_params=pltpu.CompilerParams(
            collective_id=0, has_side_effects=True, vmem_limit_bytes=60 * 2**20
        ),
        name="arnoldi",
    )(
        near_rows, near_cols, near_scale, scale_table, near_live, prev, last,
        start, leaf_basis, leaf_transfer, device_transfer, device_coupling, group_coupling, near_blocks,
    )


def solution(mesh):
    both = ("grp", "dev")
    cut = P(both, None, None)
    return jax.shard_map(
        shards,
        mesh=mesh,
        in_specs=(P(None, both), cut, P(both), P(both), P(both), P(), P(both), cut, cut, cut, P(), P()),
        out_specs=(P(None, both), P()),
        check_vma=False,
    )
```

```python
import functools

import jax
import jax.numpy as jnp
from jax import lax
from jax.experimental import pallas as pl
from jax.experimental.pallas import tpu as pltpu
from jax.sharding import PartitionSpec as P

F32 = jnp.float32
BF16 = jnp.bfloat16
HIGHEST = lax.Precision.HIGHEST
MESH = pl.DeviceIdType.MESH

R = 32
K = 64
HALF = 128
ND = 16
NG = 8
CL = 8
NB = 160
NCL = ND * CL
WIN = NCL + 16
NOFF = 30
GOFF = 6
UNROLL = 16
NPAN = 262144

NN = (((1,), (0,)), ((), ()))
NT = (((1,), (1,)), ((), ()))


def dot(a, b, dims=NN):
    return lax.dot_general(a, b, dims, precision=HIGHEST, preferred_element_type=F32)


def bdot(a, b, dims=NN):
    return lax.dot_general(a, b, dims, preferred_element_type=F32)


def split(v):
    hi = v.astype(BF16)
    return hi, (v - hi.astype(F32)).astype(BF16)


def terms(v):
    hi = v.astype(BF16)
    rest = v - hi.astype(F32)
    mid = rest.astype(BF16)
    return jnp.concatenate([hi, mid, (rest - mid.astype(F32)).astype(BF16)], axis=0)


def inner(a, b):
    p = bdot(a, b, NT)
    at = [slice(0, R), slice(R, 2 * R), slice(2 * R, 3 * R)]
    small = p[at[2], at[0]] + p[at[1], at[1]] + p[at[0], at[2]]
    return p[at[0], at[0]] + ((p[at[1], at[0]] + p[at[0], at[1]]) + small)


def combine(coeffs, blocks):
    parts = []
    for c in coeffs:
        hi = c.astype(BF16)
        rest = c - hi.astype(F32)
        mid = rest.astype(BF16)
        low = (rest - mid.astype(F32)).astype(BF16)
        zero = jnp.zeros((R, R), BF16)
        rows = [
            jnp.concatenate([hi, hi, hi], axis=1),
            jnp.concatenate([mid, mid, zero], axis=1),
            jnp.concatenate([low, zero, zero], axis=1),
        ]
        parts.append(jnp.concatenate(rows, axis=0))
    total = None
    for c, b in zip(parts, blocks):
        p = bdot(c, b)
        p = p[:R] + (p[R : 2 * R] + p[2 * R :])
        total = p if total is None else total + p
    return total


def pack(v):
    return jnp.concatenate([v[0:8], v[8:16], v[16:24], v[24:32]], axis=1)


def unpack(v):
    return jnp.concatenate([v[:, 0:32], v[:, 32:64], v[:, 64:96], v[:, 96:128]], axis=0)


def factor(gram):
    row = lax.broadcasted_iota(jnp.int32, (R, R), 0)
    col = lax.broadcasted_iota(jnp.int32, (R, R), 1)
    eye = (row == col).astype(F32)
    rid = lax.broadcasted_iota(jnp.int32, (R, 1), 0)
    m = jnp.concatenate([gram, eye], axis=1)
    for k in range(R - 1):
        pivot = m[k : k + 1, :]
        inverse = 1.0 / m[k : k + 1, k : k + 1]
        scale = jnp.where(rid > k, m[:, k : k + 1] * inverse, 0.0)
        m = m - scale * pivot
    upper = m[:, :R]
    diag = jnp.sum(jnp.where(row == col, upper, 0.0), axis=1, keepdims=True)
    rs = 1.0 / jnp.sqrt(diag)
    lower = jnp.where(row <= col, upper * rs, 0.0).T
    return lower, jnp.where(row >= col, m[:, R:] * rs, 0.0)


def permuted(c):
    return jnp.where(c < NCL, ((c >> 3) & 3) * 32 + (c >> 5) * 8 + (c & 7), c)


def num_p(h, o):
    return h * 3 + o - 1


def num_q(h, oa, j):
    return 6 + h * 12 + (oa - 1) * 4 + j


def num_z(h, s):
    return 30 + h * 2 + s


def num_ov(h):
    return 34 + h


def num_r(h, oa, j):
    return 36 + h * 12 + (oa - 1) * 4 + j


def num_v(h, o):
    return 60 + h * 3 + o - 1


QUP = 66
QDN = 67
SEM_AR1 = QDN + 1
SEM_AR2 = SEM_AR1 + ND
SEM_FAR1 = SEM_AR2 + NG
SEM_FAR2 = SEM_FAR1 + ND
NSEM = SEM_FAR2 + NG


def kernel(
    rows, cols, scl, table, live, prev, last,
    start_hbm, lbasis_hbm, ltrans_hbm, dtrans_hbm, dcoup_hbm, gcoup_hbm, blocks_hbm,
    next_ref, hess_ref,
    blocks, seg, w0, w1, t0, t1, over, ybuf, sbuf, vbuf, mbuf, gbuf, ar1, ar2,
    start, lbasis, ltrans, dtrans, dcoup, gcoup, ltcat, cah, cal, cbh, cbl, dah, dal, dbh, dbl, b1s, b2s, u, bsem, ssem, rsem,
):
    g = lax.axis_index("grp")
    d = lax.axis_index("dev")
    x, y = d // 4, d % 4
    w = (w0, w1)
    t = (t0, t1)
    ab = ((x, y), (y, x))

    def dev(h, a, b):
        return a * 4 + b if h == 0 else b * 4 + a

    def step(v, k):
        return (v + k) % 4

    pairs = (
        (start_hbm, start), (blocks_hbm, blocks), (dcoup_hbm, dcoup), (gcoup_hbm, gcoup),
        (ltrans_hbm, ltrans), (lbasis_hbm, lbasis), (dtrans_hbm, dtrans),
    )
    loads = [pltpu.make_async_copy(src, dst, bsem.at[i]) for i, (src, dst) in enumerate(pairs)]
    for i in (0, 2, 3, 4, 5, 6):
        loads[i].start()

    def remote(src, dst, number, gg, dd):
        return pltpu.make_async_remote_copy(
            src_ref=src, dst_ref=dst, send_sem=ssem.at[number], recv_sem=rsem.at[number],
            device_id=(gg, dd), device_id_type=MESH,
        )

    mbuf[...] = jnp.zeros_like(mbuf)
    gbuf[...] = jnp.zeros_like(gbuf)
    over[...] = jnp.zeros_like(over)
    for h in range(2):
        w[h][NCL:WIN] = jnp.zeros((16, R, HALF), BF16)
    seg[2 * NB] = jnp.zeros((R, 2 * HALF), F32)

    barrier = pltpu.get_barrier_semaphore()

    def greet_dev(o, c):
        pl.semaphore_signal(barrier, inc=1, device_id=(g, (d + o) % ND), device_id_type=MESH)
        return c

    def greet_grp(o, c):
        pl.semaphore_signal(barrier, inc=1, device_id=((g + o) % NG, d), device_id_type=MESH)
        return c

    lax.fori_loop(1, ND, greet_dev, 0)
    lax.fori_loop(1, NG, greet_grp, 0)

    def all_reduce(i, parts, beside=None, first=False):
        n = 8 * len(parts)
        val = jnp.concatenate([pack(p) for p in parts], axis=0) if len(parts) > 1 else pack(parts[0])
        ar1[i, d, 0:n] = val
        if first:
            pl.semaphore_wait(barrier, ND + NG - 2)

        def along_dev(o):
            return remote(ar1.at[i, d, pl.ds(0, n)], ar1.at[i, d, pl.ds(0, n)], SEM_AR1 + o, g, (d + o) % ND)

        def along_grp(o):
            return remote(ar2.at[i, g, pl.ds(0, n)], ar2.at[i, g, pl.ds(0, n)], SEM_AR2 + o, (g + o) % NG, d)

        def go(make, count):
            lax.fori_loop(1, count, lambda o, c: (make(o).start(), c)[1], 0)

        def got(make, count):
            lax.fori_loop(1, count, lambda o, c: (make(o).wait_recv(), c)[1], 0)

        def left(make, count):
            lax.fori_loop(1, count, lambda o, c: (make(o).wait_send(), c)[1], 0)

        go(along_dev, ND)
        if beside is not None:
            beside()
        got(along_dev, ND)
        total = ar1[i, 0, 0:n]
        for e in range(1, ND):
            total = total + ar1[i, e, 0:n]
        ar2[i, g, 0:n] = total
        go(along_grp, NG)
        left(along_dev, ND)
        got(along_grp, NG)
        total = ar2[i, 0, 0:n]
        for e in range(1, NG):
            total = total + ar2[i, e, 0:n]
        left(along_grp, NG)
        total = total * (1.0 / NPAN)
        return [unpack(total[8 * j : 8 * j + 8]) for j in range(len(parts))]

    def tables():
        loads[1].start()
        for i in range(2, 7):
            loads[i].wait()
        for i in range(CL // 2):
            ltcat[:, 128 * i : 128 * i + 128] = jnp.concatenate([ltrans[2 * i], ltrans[2 * i + 1]], axis=1)

        def build(src, count, ah, al, bh, bl):
            for i in range(count // 2):
                at = slice(128 * i, 128 * i + 128)
                ahead = jnp.concatenate([src[2 * i], src[2 * i + 1]], axis=1)
                ah[:, at], al[:, at] = split(ahead)
                o = count - 1 - 2 * i
                behind = jnp.concatenate([src[o], src[o - 1]], axis=0).T
                bh[:, at], bl[:, at] = split(behind)

        build(dcoup, NOFF, cah, cal, cbh, cbl)
        build(gcoup, GOFF, dah, dal, dbh, dbl)

    def far_send(i):
        return remote(
            mbuf.at[pl.ds((32 + d) * K, K)], mbuf.at[pl.ds((32 + d) * K, K)], SEM_FAR1 + i, g, (d + i) % ND
        )

    def top_send(i):
        return remote(gbuf.at[pl.ds((8 + g) * K, K)], gbuf.at[pl.ds((8 + g) * K, K)], SEM_FAR2 + i, (g + i) % NG, d)

    def shard(h, a, b):
        return w[h].at[pl.ds((a * 4 + b) * CL, CL)]

    def first(h, s):
        return (0, s) if h == 0 else (s, 0)

    def send_p(h, o):
        a, b = ab[h]
        return remote(shard(h, a, b), shard(h, a, b), num_p(h, o), g, dev(h, a, step(b, o)))

    def send_q(h, oa, j):
        a, b = ab[h]
        ref = shard(h, a, step(b, j))
        return remote(ref, ref, num_q(h, oa, j), g, dev(h, step(a, oa), b))

    def send_z(h, s):
        a, b = first(h, s)
        return remote(shard(h, a, b), w[h].at[pl.ds(NCL + s * CL, CL)], num_z(h, s), (g + NG - 1) % NG, d)

    def send_ov(h):
        return remote(t[h].at[pl.ds(NCL, 16)], over.at[h], num_ov(h), (g + 1) % NG, d)

    def send_r(h, oa, j):
        a, b = ab[h]
        src = t[h].at[pl.ds((step(a, oa) * 4 + step(b, j)) * CL, CL)]
        return remote(src, ybuf.at[h, oa - 1, j], num_r(h, oa, j), g, dev(h, step(a, oa), b))

    def send_v(h, o):
        a, b = ab[h]
        return remote(sbuf.at[h, o], vbuf.at[h, o - 1], num_v(h, o), g, dev(h, a, step(b, o)))

    def apply(v, first_call=False):
        vb = v.astype(BF16)
        for h in range(2):
            for c in range(CL):
                lo = c * 256 + h * HALF
                w[h][(ab[h][0] * 4 + ab[h][1]) * CL + c] = vb[:, lo : lo + HALF]

        for o in (1, 3, 2):
            for h in range(2):
                send_p(h, o).start()
        for oa in (1, 3, 2):
            for h in range(2):
                send_q(h, oa, 0).start()

        q = jnp.concatenate([bdot(lbasis[c], vb[:, 256 * c : 256 * c + 256], NT) for c in range(CL)], axis=0)
        coeffs = dot(ltcat[...], q)
        parents = dot(dtrans[0], coeffs)
        qh, ql = split(coeffs)
        ph, pe = split(parents)
        mbuf[pl.ds(pl.multiple_of((32 + d) * K, K), K), :] = jnp.concatenate([qh, ql, ph, pe], axis=1)

        for c in range(4):
            for h in range(2):
                b = ab[h][1]

                @pl.when(b != c)
                def _():
                    send_p(h, step(b, 4 - c)).wait_recv()
                    for oa in (1, 3, 2):
                        send_q(h, oa, step(c + 4 - b, 0)).start()

        for h in range(2):
            for s in range(2):
                sa, sb = first(h, s)
                a, b = ab[h]

                @pl.when(a != sa)
                def _():
                    send_q(h, step(a, 4 - sa), step(sb + 4 - b, 0)).wait_recv()

                @pl.when(g > 0)
                def _():
                    send_z(h, s).start()

        for h in range(2):
            a, b = ab[h]
            for oa in (1, 3, 2):
                for j in range(4):
                    from_a, from_b = step(a, 4 - oa), step(b, j)
                    if h == 0:
                        early = (from_a == 0) & (from_b < 2)
                    else:
                        early = (from_b == 0) & (from_a < 2)

                    @pl.when(jnp.logical_not(early))
                    def _():
                        send_q(h, oa, j).wait_recv()

        @pl.when(g < NG - 1)
        def _():
            for h in range(2):
                for s in range(2):
                    send_z(h, s).wait_recv()

        if first_call:
            loads[1].wait()

        lax.fori_loop(1, ND, lambda o, c: (far_send(o).start(), c)[1], 0)

        n_live = live[0]

        def near(i, carry):
            for j in range(UNROLL):
                k = i * UNROLL + j
                r, c = rows[k], cols[k]
                weight = jnp.where(k < n_live, table[scl[k]], 0.0)
                block = blocks[k]
                vc = jnp.concatenate([w0[c], w1[permuted(c)]], axis=1)
                vr = jnp.concatenate([w0[r], w1[permuted(r)]], axis=1)
                to_row = bdot(block, vc, NT).T
                to_col = bdot(vr, block)
                seg[2 * k] = seg[prev[2 * k]] + weight * to_row
                seg[2 * k + 1] = seg[prev[2 * k + 1]] + weight * to_col
            return carry

        lax.fori_loop(0, NB // UNROLL, near, 0)

        for h in range(2):
            for o in range(1, 4):
                send_p(h, o).wait_send()
                for j in range(4):
                    send_q(h, o, j).wait_send()

        @pl.when(g > 0)
        def _():
            for h in range(2):
                for s in range(2):
                    send_z(h, s).wait_send()

        for c in range(NCL, WIN):
            v = seg[last[c]]
            t0[c] = v[:, :HALF].astype(BF16)
            t1[c] = v[:, HALF:].astype(BF16)

        @pl.when(g < NG - 1)
        def _():
            for h in range(2):
                send_ov(h).start()

        def emit(i, extra):
            place = ((i // 4, i % 4), (i % 4, i // 4))
            vals = [seg[last[i * CL + c]] for c in range(CL)]
            for h in range(2):
                a, b = ab[h]
                oa, j = step(place[h][0] + 4 - a, 0), step(place[h][1] + 4 - b, 0)
                at = (place[h][0] * 4 + place[h][1]) * CL
                parts = [v[:, h * HALF : h * HALF + HALF] for v in vals]
                if extra:
                    parts = [p + over[h, i * CL + c].astype(F32) for c, p in enumerate(parts)]

                @pl.when(oa == 0)
                def _():
                    for c in range(CL):
                        sbuf[h, j, c] = parts[c]

                @pl.when(oa != 0)
                def _():
                    for c in range(CL):
                        t[h][at + c] = parts[c].astype(BF16)
                    send_r(h, oa, j).start()

        def totals(dx, dy):
            i = step(x, dx) * 4 + step(y, dy)

            @pl.when(i >= 2)
            def _():
                emit(i, False)

            return 0

        lax.fori_loop(0, 9, lambda r, c: totals(1 + r // 3, 1 + r % 3), 0)
        lax.fori_loop(1, 4, lambda r, c: totals(r, 0), 0)
        lax.fori_loop(0, 4, lambda r, c: totals(0, r), 0)

        @pl.when(g > 0)
        def _():
            for h in range(2):
                send_ov(h).wait_recv()

        for i in range(2):
            emit(i, True)

        lax.fori_loop(1, ND, lambda o, c: (far_send(o).wait_recv(), c)[1], 0)
        group_rows = pl.ds(32 * K, ND * K)
        up = remote(mbuf.at[group_rows], mbuf.at[pl.ds(16 * K, ND * K)], QUP, (g + 1) % NG, d)
        down = remote(mbuf.at[group_rows], mbuf.at[pl.ds(48 * K, ND * K)], QDN, (g + NG - 1) % NG, d)

        @pl.when(g < NG - 1)
        def _():
            up.start()

        @pl.when(g > 0)
        def _():
            down.start()

        top = mbuf[32 * K : 33 * K, :].astype(F32)
        for e in range(1, ND):
            top = top + mbuf[(32 + e) * K : (33 + e) * K, :].astype(F32)
        gh, gl = split(top[:, 64:96] + top[:, 96:128])
        gbuf[pl.ds(pl.multiple_of((8 + g) * K, K), K), :] = jnp.concatenate(
            [gh, gl, jnp.zeros((K, 64), BF16)], axis=1
        )
        lax.fori_loop(1, NG, lambda o, c: (top_send(o).start(), c)[1], 0)

        for o in (1, 3, 2, 0):
            for h in range(2):
                for oa in (1, 3, 2):
                    send_r(h, oa, o).wait_recv()
                sbuf[h, o] = sbuf[h, o] + (
                    ybuf[h, 0, o].astype(F32) + ybuf[h, 1, o].astype(F32) + ybuf[h, 2, o].astype(F32)
                )
                if o:
                    send_v(h, o).start()
        lax.fori_loop(1, NG, lambda o, c: (top_send(o).wait_recv(), c)[1], 0)

        @pl.when(g > 0)
        def _():
            up.wait_recv()

        @pl.when(g < NG - 1)
        def _():
            down.wait_recv()

        ga = gbuf[pl.ds(pl.multiple_of((10 + g) * K, K), GOFF * K), :]
        gb = gbuf[pl.ds(pl.multiple_of((1 + g) * K, K), GOFF * K), :]
        s1 = bdot(dah[...], ga) + bdot(dbh[...], gb)
        s2 = bdot(dal[...], ga) + bdot(dbl[...], gb)
        top_field = s1[:, 0:32] + s1[:, 32:64] + s2[:, 0:32]
        qa = mbuf[pl.ds(pl.multiple_of((34 + d) * K, K), NOFF * K), :]
        qb = mbuf[pl.ds(pl.multiple_of((1 + d) * K, K), NOFF * K), :]
        s1 = bdot(cah[...], qa) + bdot(cbh[...], qb)
        s2 = bdot(cal[...], qa) + bdot(cbl[...], qb)
        field = s1[:, 0:32] + s1[:, 32:64] + s2[:, 0:32]
        field_t = field.T + dot(top_field.T, dtrans[0])
        leaf_t = dot(field_t, ltcat[...])
        lh, ll = split(leaf_t)
        for c in range(CL):
            both = jnp.concatenate([lh[:, K * c : K * c + K], ll[:, K * c : K * c + K]], axis=0)
            far = bdot(both, lbasis[c])
            u[:, 256 * c : 256 * c + 256] = far[:R] + far[R:]

        lax.fori_loop(1, ND, lambda o, c: (far_send(o).wait_send(), c)[1], 0)
        lax.fori_loop(1, NG, lambda o, c: (top_send(o).wait_send(), c)[1], 0)
        @pl.when(g < NG - 1)
        def _():
            up.wait_send()

        @pl.when(g > 0)
        def _():
            down.wait_send()

        for h in range(2):
            for o in (1, 3, 2):
                send_v(h, o).wait_recv()
            for c in range(CL):
                total = sbuf[h, 0, c] + vbuf[h, 0, c] + vbuf[h, 1, c] + vbuf[h, 2, c]
                lo = 256 * c + h * HALF
                u[:, lo : lo + HALF] = u[:, lo : lo + HALF] + total
        for h in range(2):
            for o in range(1, 4):
                send_v(h, o).wait_send()
                for j in range(4):
                    send_r(h, o, j).wait_send()

        @pl.when(g < NG - 1)
        def _():
            for h in range(2):
                send_ov(h).wait_send()

    row = lax.broadcasted_iota(jnp.int32, (R, R), 0)
    col = lax.broadcasted_iota(jnp.int32, (R, R), 1)
    half_eye = jnp.where(row == col, 0.5, 0.0)

    tn = (((0,), (0,)), ((), ()))
    loads[0].wait()
    ss = terms(start[...])
    (gram,) = all_reduce(0, [inner(ss, ss)], beside=tables, first=True)
    _, inverse = factor(gram)
    v = combine([inverse], [ss])
    b1s[...] = terms(v)
    apply(v, first_call=True)

    us = terms(u[...])
    ha, gram = all_reduce(1, [inner(b1s[...], us), inner(us, us)])
    lower1, inverse = factor(gram - dot(ha, ha, tn))
    v = combine([inverse, -dot(inverse, ha, NT)], [us, b1s[...]])
    b2s[...] = terms(v)
    hess_ref[0] = ha + half_eye
    hess_ref[1] = lower1
    apply(v)

    us = terms(u[...])
    hb, hc, gram = all_reduce(2, [inner(b1s[...], us), inner(b2s[...], us), inner(us, us)])
    lower2, inverse = factor(gram - dot(hb, hb, tn) - dot(hc, hc, tn))
    next_ref[...] = combine(
        [inverse, -dot(inverse, hb, NT), -dot(inverse, hc, NT)], [us, b1s[...], b2s[...]]
    )
    hess_ref[2] = hb
    hess_ref[3] = hc + half_eye
    hess_ref[4] = lower2


def chains(near_rows, near_cols):
    target = jnp.stack([near_rows, near_cols], axis=1).reshape(-1)
    order = jnp.arange(2 * NB, dtype=jnp.int32)
    before = (target[:, None] == target[None, :]) & (order[None, :] < order[:, None])
    prev = jnp.max(jnp.where(before, order[None, :], -1), axis=1)
    hit = jnp.arange(WIN, dtype=jnp.int32)[:, None] == target[None, :]
    last = jnp.max(jnp.where(hit, order[None, :], -1), axis=1)
    return jnp.where(prev < 0, 2 * NB, prev), jnp.where(last < 0, 2 * NB, last)


def shards(
    start, near_blocks, near_rows, near_cols, near_scale, scale_table, near_live,
    leaf_basis, leaf_transfer, device_transfer, device_coupling, group_coupling,
):
    prev, last = chains(near_rows, near_cols)
    smem = pl.BlockSpec(memory_space=pltpu.SMEM)
    vmem = pl.BlockSpec(memory_space=pltpu.VMEM)
    anywhere = pl.BlockSpec(memory_space=pltpu.HBM)
    outs = (jax.ShapeDtypeStruct((R, 2048), F32), jax.ShapeDtypeStruct((5, R, R), F32))
    return pl.pallas_call(
        kernel,
        out_shape=outs,
        in_specs=[smem] * 7 + [anywhere] * 7,
        out_specs=(vmem, vmem),
        scratch_shapes=[
            pltpu.VMEM((NB, 256, 256), BF16),
            pltpu.VMEM((2 * NB + 1, R, 256), F32),
            pltpu.VMEM((WIN, R, HALF), BF16),
            pltpu.VMEM((WIN, R, HALF), BF16),
            pltpu.VMEM((WIN, R, HALF), BF16),
            pltpu.VMEM((WIN, R, HALF), BF16),
            pltpu.VMEM((2, 16, R, HALF), BF16),
            pltpu.VMEM((2, 3, 4, CL, R, HALF), BF16),
            pltpu.VMEM((2, 4, CL, R, HALF), F32),
            pltpu.VMEM((2, 3, CL, R, HALF), F32),
            pltpu.VMEM((80 * K, 128), BF16),
            pltpu.VMEM((24 * K, 128), BF16),
            pltpu.VMEM((3, ND, 24, 128), F32),
            pltpu.VMEM((3, NG, 24, 128), F32),
            pltpu.VMEM((R, 2048), F32),
            pltpu.VMEM((CL, K, 256), BF16),
            pltpu.VMEM((CL, K, K), F32),
            pltpu.VMEM((1, K, K), F32),
            pltpu.VMEM((NOFF, K, K), F32),
            pltpu.VMEM((GOFF, K, K), F32),
            pltpu.VMEM((K, CL * K), F32),
            pltpu.VMEM((K, NOFF * K), BF16),
            pltpu.VMEM((K, NOFF * K), BF16),
            pltpu.VMEM((K, NOFF * K), BF16),
            pltpu.VMEM((K, NOFF * K), BF16),
            pltpu.VMEM((K, GOFF * K), BF16),
            pltpu.VMEM((K, GOFF * K), BF16),
            pltpu.VMEM((K, GOFF * K), BF16),
            pltpu.VMEM((K, GOFF * K), BF16),
            pltpu.VMEM((3 * R, 2048), BF16),
            pltpu.VMEM((3 * R, 2048), BF16),
            pltpu.VMEM((R, 2048), F32),
            pltpu.SemaphoreType.DMA((7,)),
            pltpu.SemaphoreType.DMA((NSEM,)),
            pltpu.SemaphoreType.DMA((NSEM,)),
        ],
        compiler_params=pltpu.CompilerParams(
            collective_id=0, has_side_effects=True, vmem_limit_bytes=60 * 2**20
        ),
        name="arnoldi",
    )(
        near_rows, near_cols, near_scale, scale_table, near_live, prev, last,
        start, leaf_basis, leaf_transfer, device_transfer, device_coupling, group_coupling, near_blocks,
    )


def solution(mesh):
    both = ("grp", "dev")
    cut = P(both, None, None)
    return jax.shard_map(
        shards,
        mesh=mesh,
        in_specs=(P(None, both), cut, P(both), P(both), P(both), P(), P(both), cut, cut, cut, P(), P()),
        out_specs=(P(None, both), P()),
        check_vma=False,
    )
```

```python
import functools

import jax
import jax.numpy as jnp
from jax import lax
from jax.experimental import pallas as pl
from jax.experimental.pallas import tpu as pltpu
from jax.sharding import PartitionSpec as P

F32 = jnp.float32
BF16 = jnp.bfloat16
HIGHEST = lax.Precision.HIGHEST
MESH = pl.DeviceIdType.MESH

R = 32
RB = 16
K = 64
HALF = 128
ND = 16
NG = 8
CL = 8
NB = 160
NCL = ND * CL
WIN = NCL + 16
NOFF = 30
GOFF = 6
UNROLL = 16
NPAN = 262144

NN = (((1,), (0,)), ((), ()))
NT = (((1,), (1,)), ((), ()))


def dot(a, b, dims=NN):
    return lax.dot_general(a, b, dims, precision=HIGHEST, preferred_element_type=F32)


def bdot(a, b, dims=NN):
    return lax.dot_general(a, b, dims, preferred_element_type=F32)


def split(v):
    hi = v.astype(BF16)
    return hi, (v - hi.astype(F32)).astype(BF16)


def terms(v):
    hi = v.astype(BF16)
    rest = v - hi.astype(F32)
    mid = rest.astype(BF16)
    return jnp.concatenate([hi, mid, (rest - mid.astype(F32)).astype(BF16)], axis=0)


def inner(a, b):
    p = bdot(a, b, NT)
    at = [slice(0, R), slice(R, 2 * R), slice(2 * R, 3 * R)]
    small = p[at[2], at[0]] + p[at[1], at[1]] + p[at[0], at[2]]
    return p[at[0], at[0]] + ((p[at[1], at[0]] + p[at[0], at[1]]) + small)


def combine(coeffs, blocks):
    parts = []
    for c in coeffs:
        hi = c.astype(BF16)
        rest = c - hi.astype(F32)
        mid = rest.astype(BF16)
        low = (rest - mid.astype(F32)).astype(BF16)
        zero = jnp.zeros((R, R), BF16)
        rows = [
            jnp.concatenate([hi, hi, hi], axis=1),
            jnp.concatenate([mid, mid, zero], axis=1),
            jnp.concatenate([low, zero, zero], axis=1),
        ]
        parts.append(jnp.concatenate(rows, axis=0))
    total = None
    for c, b in zip(parts, blocks):
        p = bdot(c, b)
        p = p[:R] + (p[R : 2 * R] + p[2 * R :])
        total = p if total is None else total + p
    return total


def pack(v):
    return jnp.concatenate([v[0:8], v[8:16], v[16:24], v[24:32]], axis=1)


def unpack(v):
    return jnp.concatenate([v[:, 0:32], v[:, 32:64], v[:, 64:96], v[:, 96:128]], axis=0)


def factor(gram):
    row = lax.broadcasted_iota(jnp.int32, (R, R), 0)
    col = lax.broadcasted_iota(jnp.int32, (R, R), 1)
    eye = (row == col).astype(F32)
    rid = lax.broadcasted_iota(jnp.int32, (R, 1), 0)
    m = jnp.concatenate([gram, eye], axis=1)
    for k in range(R - 1):
        pivot = m[k : k + 1, :]
        inverse = 1.0 / m[k : k + 1, k : k + 1]
        scale = jnp.where(rid > k, m[:, k : k + 1] * inverse, 0.0)
        m = m - scale * pivot
    upper = m[:, :R]
    diag = jnp.sum(jnp.where(row == col, upper, 0.0), axis=1, keepdims=True)
    rs = 1.0 / jnp.sqrt(diag)
    lower = jnp.where(row <= col, upper * rs, 0.0).T
    return lower, jnp.where(row >= col, m[:, R:] * rs, 0.0)


def permuted(c):
    return jnp.where(c < NCL, ((c >> 3) & 3) * 32 + (c >> 5) * 8 + (c & 7), c)


PER = 66


def num_p(p, h, o):
    return p * PER + h * 3 + o - 1


def num_q(p, h, oa, j):
    return p * PER + 6 + h * 12 + (oa - 1) * 4 + j


def num_z(p, h, s):
    return p * PER + 30 + h * 2 + s


def num_ov(p, h):
    return p * PER + 34 + h


def num_r(p, h, oa, j):
    return p * PER + 36 + h * 12 + (oa - 1) * 4 + j


def num_v(p, h, o):
    return p * PER + 60 + h * 3 + o - 1


QUP = 2 * PER
QDN = QUP + 1
SEM_AR1 = QDN + 1
SEM_AR2 = SEM_AR1 + ND
SEM_FAR1 = SEM_AR2 + NG
SEM_FAR2 = SEM_FAR1 + ND
NSEM = SEM_FAR2 + NG


def kernel(
    rows, cols, scl, table, live, prev, last,
    start_hbm, lbasis_hbm, ltrans_hbm, dtrans_hbm, dcoup_hbm, gcoup_hbm, blocks_hbm,
    next_ref, hess_ref,
    blocks, segc, segr0, segr1, w00, w01, w10, w11, t00, t01, t10, t11, over, ybuf, sbuf, vbuf, mbuf, gbuf, ar1, ar2,
    start, lbasis, ltrans, dtrans, dcoup, gcoup, ltcat, cah, cal, cbh, cbl, dah, dal, dbh, dbl, b1s, b2s, u, bsem, ssem, rsem,
):
    g = lax.axis_index("grp")
    d = lax.axis_index("dev")
    x, y = d // 4, d % 4
    segr = (segr0, segr1)
    w = ((w00, w01), (w10, w11))
    t = ((t00, t01), (t10, t11))
    ab = ((x, y), (y, x))

    def dev(h, a, b):
        return a * 4 + b if h == 0 else b * 4 + a

    def step(v, k):
        return (v + k) % 4

    pairs = (
        (start_hbm, start), (blocks_hbm, blocks), (dcoup_hbm, dcoup), (gcoup_hbm, gcoup),
        (ltrans_hbm, ltrans), (lbasis_hbm, lbasis), (dtrans_hbm, dtrans),
    )
    loads = [pltpu.make_async_copy(src, dst, bsem.at[i]) for i, (src, dst) in enumerate(pairs)]
    for i in (0, 2, 3, 4, 5, 6):
        loads[i].start()

    def remote(src, dst, number, gg, dd):
        return pltpu.make_async_remote_copy(
            src_ref=src, dst_ref=dst, send_sem=ssem.at[number], recv_sem=rsem.at[number],
            device_id=(gg, dd), device_id_type=MESH,
        )

    mbuf[...] = jnp.zeros_like(mbuf)
    gbuf[...] = jnp.zeros_like(gbuf)
    over[...] = jnp.zeros_like(over)
    for p in range(2):
        for h in range(2):
            w[p][h][NCL:WIN] = jnp.zeros((16, RB, HALF), BF16)
        segr[p][NB] = jnp.zeros((R, HALF), F32)
    segc[NB] = jnp.zeros((R, 2 * HALF), F32)

    barrier = pltpu.get_barrier_semaphore()

    def greet_dev(o, c):
        pl.semaphore_signal(barrier, inc=1, device_id=(g, (d + o) % ND), device_id_type=MESH)
        return c

    def greet_grp(o, c):
        pl.semaphore_signal(barrier, inc=1, device_id=((g + o) % NG, d), device_id_type=MESH)
        return c

    lax.fori_loop(1, ND, greet_dev, 0)
    lax.fori_loop(1, NG, greet_grp, 0)

    def all_reduce(i, parts, beside=None, first=False):
        n = 8 * len(parts)
        val = jnp.concatenate([pack(p) for p in parts], axis=0) if len(parts) > 1 else pack(parts[0])
        ar1[i, d, 0:n] = val
        if first:
            pl.semaphore_wait(barrier, ND + NG - 2)

        def along_dev(o):
            return remote(ar1.at[i, d, pl.ds(0, n)], ar1.at[i, d, pl.ds(0, n)], SEM_AR1 + o, g, (d + o) % ND)

        def along_grp(o):
            return remote(ar2.at[i, g, pl.ds(0, n)], ar2.at[i, g, pl.ds(0, n)], SEM_AR2 + o, (g + o) % NG, d)

        def go(make, count):
            lax.fori_loop(1, count, lambda o, c: (make(o).start(), c)[1], 0)

        def got(make, count):
            lax.fori_loop(1, count, lambda o, c: (make(o).wait_recv(), c)[1], 0)

        def left(make, count):
            lax.fori_loop(1, count, lambda o, c: (make(o).wait_send(), c)[1], 0)

        go(along_dev, ND)
        if beside is not None:
            beside()
        got(along_dev, ND)
        total = ar1[i, 0, 0:n]
        for e in range(1, ND):
            total = total + ar1[i, e, 0:n]
        ar2[i, g, 0:n] = total
        go(along_grp, NG)
        left(along_dev, ND)
        got(along_grp, NG)
        total = ar2[i, 0, 0:n]
        for e in range(1, NG):
            total = total + ar2[i, e, 0:n]
        left(along_grp, NG)
        total = total * (1.0 / NPAN)
        return [unpack(total[8 * j : 8 * j + 8]) for j in range(len(parts))]

    def tables():
        loads[1].start()
        for i in range(2, 7):
            loads[i].wait()
        for i in range(CL // 2):
            ltcat[:, 128 * i : 128 * i + 128] = jnp.concatenate([ltrans[2 * i], ltrans[2 * i + 1]], axis=1)

        def build(src, count, ah, al, bh, bl):
            for i in range(count // 2):
                at = slice(128 * i, 128 * i + 128)
                ahead = jnp.concatenate([src[2 * i], src[2 * i + 1]], axis=1)
                ah[:, at], al[:, at] = split(ahead)
                o = count - 1 - 2 * i
                behind = jnp.concatenate([src[o], src[o - 1]], axis=0).T
                bh[:, at], bl[:, at] = split(behind)

        build(dcoup, NOFF, cah, cal, cbh, cbl)
        build(gcoup, GOFF, dah, dal, dbh, dbl)

    def far_send(i):
        return remote(
            mbuf.at[pl.ds((32 + d) * K, K)], mbuf.at[pl.ds((32 + d) * K, K)], SEM_FAR1 + i, g, (d + i) % ND
        )

    def top_send(i):
        return remote(gbuf.at[pl.ds((8 + g) * K, K)], gbuf.at[pl.ds((8 + g) * K, K)], SEM_FAR2 + i, (g + i) % NG, d)

    def shard(p, h, a, b):
        return w[p][h].at[pl.ds((a * 4 + b) * CL, CL)]

    def first(h, s):
        return (0, s) if h == 0 else (s, 0)

    def send_p(p, h, o):
        a, b = ab[h]
        return remote(shard(p, h, a, b), shard(p, h, a, b), num_p(p, h, o), g, dev(h, a, step(b, o)))

    def send_q(p, h, oa, j):
        a, b = ab[h]
        ref = shard(p, h, a, step(b, j))
        return remote(ref, ref, num_q(p, h, oa, j), g, dev(h, step(a, oa), b))

    def send_z(p, h, s):
        a, b = first(h, s)
        return remote(
            shard(p, h, a, b), w[p][h].at[pl.ds(NCL + s * CL, CL)], num_z(p, h, s), (g + NG - 1) % NG, d
        )

    def send_ov(p, h):
        return remote(t[p][h].at[pl.ds(NCL, 16)], over.at[p, h], num_ov(p, h), (g + 1) % NG, d)

    def send_r(p, h, oa, j):
        a, b = ab[h]
        src = t[p][h].at[pl.ds((step(a, oa) * 4 + step(b, j)) * CL, CL)]
        return remote(src, ybuf.at[p, h, oa - 1, j], num_r(p, h, oa, j), g, dev(h, step(a, oa), b))

    def send_v(p, h, o):
        a, b = ab[h]
        return remote(sbuf.at[p, h, o], vbuf.at[p, h, o - 1], num_v(p, h, o), g, dev(h, a, step(b, o)))

    def apply(v, first_call=False):
        vb = v.astype(BF16)
        for p in range(2):
            for h in range(2):
                for c in range(CL):
                    lo = c * 256 + p * HALF
                    w[p][h][(ab[h][0] * 4 + ab[h][1]) * CL + c] = vb[h * RB : h * RB + RB, lo : lo + HALF]

        def along_b(p):
            for o in (1, 3, 2):
                for h in range(2):
                    send_p(p, h, o).start()

        def own_along_a(p):
            for oa in (1, 3, 2):
                for h in range(2):
                    send_q(p, h, oa, 0).start()

        def along_a(p):
            for c in range(4):
                for h in range(2):
                    b = ab[h][1]

                    @pl.when(b != c)
                    def _():
                        send_p(p, h, step(b, 4 - c)).wait_recv()
                        for oa in (1, 3, 2):
                            send_q(p, h, oa, step(c + 4 - b, 0)).start()

        def pass_on(p):
            for h in range(2):
                for s in range(2):
                    sa, sb = first(h, s)
                    a, b = ab[h]

                    @pl.when(a != sa)
                    def _():
                        send_q(p, h, step(a, 4 - sa), step(sb + 4 - b, 0)).wait_recv()

                    @pl.when(g > 0)
                    def _():
                        send_z(p, h, s).start()

        def gathered(p):
            for h in range(2):
                a, b = ab[h]
                for oa in (1, 3, 2):
                    for j in range(4):
                        from_a, from_b = step(a, 4 - oa), step(b, j)
                        if h == 0:
                            early = (from_a == 0) & (from_b < 2)
                        else:
                            early = (from_b == 0) & (from_a < 2)

                        @pl.when(jnp.logical_not(early))
                        def _():
                            send_q(p, h, oa, j).wait_recv()

            @pl.when(g < NG - 1)
            def _():
                for h in range(2):
                    for s in range(2):
                        send_z(p, h, s).wait_recv()

        n_live = live[0]

        def panels(p, c):
            return jnp.concatenate([w[p][0][c], w[p][1][permuted(c)]], axis=0)

        def loop(one):
            def some(i, carry):
                for j in range(UNROLL):
                    k = i * UNROLL + j
                    one(k, jnp.where(k < n_live, table[scl[k]], 0.0))
                return carry

            lax.fori_loop(0, NB // UNROLL, some, 0)

        def near_first(k, weight):
            segc[k] = bdot(panels(0, rows[k]), blocks[k, 0:HALF])

        def near_second(k, weight):
            to_col = segc[k] + bdot(panels(1, rows[k]), blocks[k, HALF : 2 * HALF])
            segc[k] = segc[prev[1, k]] + weight * to_col
            near_row(0, k, weight)

        def near_row(p, k, weight):
            c = cols[k]
            both = jnp.concatenate([panels(0, c), panels(1, c)], axis=1)
            to_row = bdot(blocks[k, p * HALF : p * HALF + HALF], both, NT).T
            segr[p][k] = segr[p][prev[0, k]] + weight * to_row

        def near_total(p, c):
            return segr[p][last[0, c]] + segc[last[1, c], :, p * HALF : p * HALF + HALF]

        def emit(p, i, extra):
            place = ((i // 4, i % 4), (i % 4, i // 4))
            vals = [near_total(p, i * CL + c) for c in range(CL)]
            for h in range(2):
                a, b = ab[h]
                oa, j = step(place[h][0] + 4 - a, 0), step(place[h][1] + 4 - b, 0)
                at = (place[h][0] * 4 + place[h][1]) * CL
                parts = [v[h * RB : h * RB + RB] for v in vals]
                if extra:
                    parts = [v + over[p, h, i * CL + c].astype(F32) for c, v in enumerate(parts)]

                @pl.when(oa == 0)
                def _():
                    for c in range(CL):
                        sbuf[p, h, j, c] = parts[c]

                @pl.when(oa != 0)
                def _():
                    for c in range(CL):
                        t[p][h][at + c] = parts[c].astype(BF16)
                    send_r(p, h, oa, j).start()

        def overflow(p):
            for c in range(NCL, WIN):
                v = near_total(p, c)
                t[p][0][c] = v[:RB].astype(BF16)
                t[p][1][c] = v[RB:].astype(BF16)

            @pl.when(g < NG - 1)
            def _():
                for h in range(2):
                    send_ov(p, h).start()

        def totals(p):
            def one(dx, dy):
                i = step(x, dx) * 4 + step(y, dy)

                @pl.when(i >= 2)
                def _():
                    emit(p, i, False)

                return 0

            lax.fori_loop(0, 9, lambda r, c: one(1 + r // 3, 1 + r % 3), 0)
            lax.fori_loop(1, 4, lambda r, c: one(r, 0), 0)
            lax.fori_loop(0, 4, lambda r, c: one(0, r), 0)

        def first_shards(p):
            @pl.when(g > 0)
            def _():
                for h in range(2):
                    send_ov(p, h).wait_recv()

            for i in range(2):
                emit(p, i, True)

        def summed(p):
            for o in (1, 3, 2, 0):
                for h in range(2):
                    for oa in (1, 3, 2):
                        send_r(p, h, oa, o).wait_recv()
                    sbuf[p, h, o] = sbuf[p, h, o] + (
                        ybuf[p, h, 0, o].astype(F32) + ybuf[p, h, 1, o].astype(F32) + ybuf[p, h, 2, o].astype(F32)
                    )
                    if o:
                        send_v(p, h, o).start()

        along_b(0)
        own_along_a(0)
        along_b(1)

        q = jnp.concatenate([bdot(lbasis[c], vb[:, 256 * c : 256 * c + 256], NT) for c in range(CL)], axis=0)
        coeffs = dot(ltcat[...], q)
        parents = dot(dtrans[0], coeffs)
        qh, ql = split(coeffs)
        ph, pe = split(parents)
        mbuf[pl.ds(pl.multiple_of((32 + d) * K, K), K), :] = jnp.concatenate([qh, ql, ph, pe], axis=1)

        along_a(0)
        pass_on(0)
        own_along_a(1)
        along_a(1)
        gathered(0)
        if first_call:
            loads[1].wait()
        loop(near_first)
        pass_on(1)
        gathered(1)
        lax.fori_loop(1, ND, lambda o, c: (far_send(o).start(), c)[1], 0)
        loop(near_second)
        overflow(0)
        totals(0)
        loop(lambda k, weight: near_row(1, k, weight))
        overflow(1)
        totals(1)
        first_shards(0)

        lax.fori_loop(1, ND, lambda o, c: (far_send(o).wait_recv(), c)[1], 0)
        group_rows = pl.ds(32 * K, ND * K)
        up = remote(mbuf.at[group_rows], mbuf.at[pl.ds(16 * K, ND * K)], QUP, (g + 1) % NG, d)
        down = remote(mbuf.at[group_rows], mbuf.at[pl.ds(48 * K, ND * K)], QDN, (g + NG - 1) % NG, d)

        @pl.when(g < NG - 1)
        def _():
            up.start()

        @pl.when(g > 0)
        def _():
            down.start()

        top = mbuf[32 * K : 33 * K, :].astype(F32)
        for e in range(1, ND):
            top = top + mbuf[(32 + e) * K : (33 + e) * K, :].astype(F32)
        gh, gl = split(top[:, 64:96] + top[:, 96:128])
        gbuf[pl.ds(pl.multiple_of((8 + g) * K, K), K), :] = jnp.concatenate(
            [gh, gl, jnp.zeros((K, 64), BF16)], axis=1
        )
        lax.fori_loop(1, NG, lambda o, c: (top_send(o).start(), c)[1], 0)

        first_shards(1)
        summed(0)
        summed(1)

        lax.fori_loop(1, NG, lambda o, c: (top_send(o).wait_recv(), c)[1], 0)

        @pl.when(g > 0)
        def _():
            up.wait_recv()

        @pl.when(g < NG - 1)
        def _():
            down.wait_recv()

        ga = gbuf[pl.ds(pl.multiple_of((10 + g) * K, K), GOFF * K), :]
        gb = gbuf[pl.ds(pl.multiple_of((1 + g) * K, K), GOFF * K), :]
        s1 = bdot(dah[...], ga) + bdot(dbh[...], gb)
        s2 = bdot(dal[...], ga) + bdot(dbl[...], gb)
        top_field = s1[:, 0:32] + s1[:, 32:64] + s2[:, 0:32]
        qa = mbuf[pl.ds(pl.multiple_of((34 + d) * K, K), NOFF * K), :]
        qb = mbuf[pl.ds(pl.multiple_of((1 + d) * K, K), NOFF * K), :]
        s1 = bdot(cah[...], qa) + bdot(cbh[...], qb)
        s2 = bdot(cal[...], qa) + bdot(cbl[...], qb)
        field = s1[:, 0:32] + s1[:, 32:64] + s2[:, 0:32]
        field_t = field.T + dot(top_field.T, dtrans[0])
        leaf_t = dot(field_t, ltcat[...])
        lh, ll = split(leaf_t)
        for c in range(CL):
            both = jnp.concatenate([lh[:, K * c : K * c + K], ll[:, K * c : K * c + K]], axis=0)
            far = bdot(both, lbasis[c])
            u[:, 256 * c : 256 * c + 256] = far[:R] + far[R:]

        lax.fori_loop(1, ND, lambda o, c: (far_send(o).wait_send(), c)[1], 0)
        lax.fori_loop(1, NG, lambda o, c: (top_send(o).wait_send(), c)[1], 0)
        @pl.when(g < NG - 1)
        def _():
            up.wait_send()

        @pl.when(g > 0)
        def _():
            down.wait_send()

        for p in range(2):
            for h in range(2):
                for o in (1, 3, 2):
                    send_v(p, h, o).wait_recv()
                for c in range(CL):
                    total = sbuf[p, h, 0, c] + vbuf[p, h, 0, c] + vbuf[p, h, 1, c] + vbuf[p, h, 2, c]
                    at = (slice(h * RB, h * RB + RB), slice(256 * c + p * HALF, 256 * c + p * HALF + HALF))
                    u[at] = u[at] + total

        for p in range(2):
            for h in range(2):
                for o in range(1, 4):
                    send_p(p, h, o).wait_send()
                    send_v(p, h, o).wait_send()
                    for j in range(4):
                        send_q(p, h, o, j).wait_send()
                        send_r(p, h, o, j).wait_send()

                @pl.when(g > 0)
                def _():
                    for s in range(2):
                        send_z(p, h, s).wait_send()

                @pl.when(g < NG - 1)
                def _():
                    send_ov(p, h).wait_send()

    row = lax.broadcasted_iota(jnp.int32, (R, R), 0)
    col = lax.broadcasted_iota(jnp.int32, (R, R), 1)
    half_eye = jnp.where(row == col, 0.5, 0.0)

    tn = (((0,), (0,)), ((), ()))
    loads[0].wait()
    ss = terms(start[...])
    (gram,) = all_reduce(0, [inner(ss, ss)], beside=tables, first=True)
    _, inverse = factor(gram)
    v = combine([inverse], [ss])
    b1s[...] = terms(v)
    apply(v, first_call=True)

    us = terms(u[...])
    ha, gram = all_reduce(1, [inner(b1s[...], us), inner(us, us)])
    lower1, inverse = factor(gram - dot(ha, ha, tn))
    v = combine([inverse, -dot(inverse, ha, NT)], [us, b1s[...]])
    b2s[...] = terms(v)
    hess_ref[0] = ha + half_eye
    hess_ref[1] = lower1
    apply(v)

    us = terms(u[...])
    hb, hc, gram = all_reduce(2, [inner(b1s[...], us), inner(b2s[...], us), inner(us, us)])
    lower2, inverse = factor(gram - dot(hb, hb, tn) - dot(hc, hc, tn))
    next_ref[...] = combine(
        [inverse, -dot(inverse, hb, NT), -dot(inverse, hc, NT)], [us, b1s[...], b2s[...]]
    )
    hess_ref[2] = hb
    hess_ref[3] = hc + half_eye
    hess_ref[4] = lower2


def chains(near_rows, near_cols):
    target = jnp.stack([near_rows, near_cols])
    order = jnp.arange(NB, dtype=jnp.int32)
    before = (target[:, :, None] == target[:, None, :]) & (order[None, :] < order[:, None])[None]
    prev = jnp.max(jnp.where(before, order, -1), axis=2)
    hit = jnp.arange(WIN, dtype=jnp.int32)[None, :, None] == target[:, None, :]
    last = jnp.max(jnp.where(hit, order, -1), axis=2)
    return jnp.where(prev < 0, NB, prev), jnp.where(last < 0, NB, last)


def shards(
    start, near_blocks, near_rows, near_cols, near_scale, scale_table, near_live,
    leaf_basis, leaf_transfer, device_transfer, device_coupling, group_coupling,
):
    prev, last = chains(near_rows, near_cols)
    smem = pl.BlockSpec(memory_space=pltpu.SMEM)
    vmem = pl.BlockSpec(memory_space=pltpu.VMEM)
    anywhere = pl.BlockSpec(memory_space=pltpu.HBM)
    outs = (jax.ShapeDtypeStruct((R, 2048), F32), jax.ShapeDtypeStruct((5, R, R), F32))
    return pl.pallas_call(
        kernel,
        out_shape=outs,
        in_specs=[smem] * 7 + [anywhere] * 7,
        out_specs=(vmem, vmem),
        scratch_shapes=[
            pltpu.VMEM((NB, 256, 256), BF16),
            pltpu.VMEM((NB + 1, R, 256), F32),
            pltpu.VMEM((NB + 1, R, HALF), F32),
            pltpu.VMEM((NB + 1, R, HALF), F32),
            pltpu.VMEM((WIN, RB, HALF), BF16),
            pltpu.VMEM((WIN, RB, HALF), BF16),
            pltpu.VMEM((WIN, RB, HALF), BF16),
            pltpu.VMEM((WIN, RB, HALF), BF16),
            pltpu.VMEM((WIN, RB, HALF), BF16),
            pltpu.VMEM((WIN, RB, HALF), BF16),
            pltpu.VMEM((WIN, RB, HALF), BF16),
            pltpu.VMEM((WIN, RB, HALF), BF16),
            pltpu.VMEM((2, 2, 16, RB, HALF), BF16),
            pltpu.VMEM((2, 2, 3, 4, CL, RB, HALF), BF16),
            pltpu.VMEM((2, 2, 4, CL, RB, HALF), F32),
            pltpu.VMEM((2, 2, 3, CL, RB, HALF), F32),
            pltpu.VMEM((80 * K, 128), BF16),
            pltpu.VMEM((24 * K, 128), BF16),
            pltpu.VMEM((3, ND, 24, 128), F32),
            pltpu.VMEM((3, NG, 24, 128), F32),
            pltpu.VMEM((R, 2048), F32),
            pltpu.VMEM((CL, K, 256), BF16),
            pltpu.VMEM((CL, K, K), F32),
            pltpu.VMEM((1, K, K), F32),
            pltpu.VMEM((NOFF, K, K), F32),
            pltpu.VMEM((GOFF, K, K), F32),
            pltpu.VMEM((K, CL * K), F32),
            pltpu.VMEM((K, NOFF * K), BF16),
            pltpu.VMEM((K, NOFF * K), BF16),
            pltpu.VMEM((K, NOFF * K), BF16),
            pltpu.VMEM((K, NOFF * K), BF16),
            pltpu.VMEM((K, GOFF * K), BF16),
            pltpu.VMEM((K, GOFF * K), BF16),
            pltpu.VMEM((K, GOFF * K), BF16),
            pltpu.VMEM((K, GOFF * K), BF16),
            pltpu.VMEM((3 * R, 2048), BF16),
            pltpu.VMEM((3 * R, 2048), BF16),
            pltpu.VMEM((R, 2048), F32),
            pltpu.SemaphoreType.DMA((7,)),
            pltpu.SemaphoreType.DMA((NSEM,)),
            pltpu.SemaphoreType.DMA((NSEM,)),
        ],
        compiler_params=pltpu.CompilerParams(
            collective_id=0, has_side_effects=True, vmem_limit_bytes=60 * 2**20
        ),
        name="arnoldi",
    )(
        near_rows, near_cols, near_scale, scale_table, near_live, prev, last,
        start, leaf_basis, leaf_transfer, device_transfer, device_coupling, group_coupling, near_blocks,
    )


def solution(mesh):
    both = ("grp", "dev")
    cut = P(both, None, None)
    return jax.shard_map(
        shards,
        mesh=mesh,
        in_specs=(P(None, both), cut, P(both), P(both), P(both), P(), P(both), cut, cut, cut, P(), P()),
        out_specs=(P(None, both), P()),
        check_vma=False,
    )
```

```python
import functools

import jax
import jax.numpy as jnp
from jax import lax
from jax.experimental import pallas as pl
from jax.experimental.pallas import tpu as pltpu
from jax.sharding import PartitionSpec as P

F32 = jnp.float32
BF16 = jnp.bfloat16
HIGHEST = lax.Precision.HIGHEST
MESH = pl.DeviceIdType.MESH

R = 32
RB = 16
K = 64
HALF = 128
ND = 16
NG = 8
CL = 8
NB = 160
NCL = ND * CL
WIN = NCL + 16
NOFF = 30
GOFF = 6
UNROLL = 16
NPAN = 262144

NN = (((1,), (0,)), ((), ()))
NT = (((1,), (1,)), ((), ()))


def dot(a, b, dims=NN):
    return lax.dot_general(a, b, dims, precision=HIGHEST, preferred_element_type=F32)


def bdot(a, b, dims=NN):
    return lax.dot_general(a, b, dims, preferred_element_type=F32)


def split(v):
    hi = v.astype(BF16)
    return hi, (v - hi.astype(F32)).astype(BF16)


def terms(v):
    hi = v.astype(BF16)
    rest = v - hi.astype(F32)
    mid = rest.astype(BF16)
    return jnp.concatenate([hi, mid, (rest - mid.astype(F32)).astype(BF16)], axis=0)


def inner(a, b):
    p = bdot(a, b, NT)
    at = [slice(0, R), slice(R, 2 * R), slice(2 * R, 3 * R)]
    small = p[at[2], at[0]] + p[at[1], at[1]] + p[at[0], at[2]]
    return p[at[0], at[0]] + ((p[at[1], at[0]] + p[at[0], at[1]]) + small)


def combine(coeffs, blocks):
    parts = []
    for c in coeffs:
        hi = c.astype(BF16)
        rest = c - hi.astype(F32)
        mid = rest.astype(BF16)
        low = (rest - mid.astype(F32)).astype(BF16)
        zero = jnp.zeros((R, R), BF16)
        rows = [
            jnp.concatenate([hi, hi, hi], axis=1),
            jnp.concatenate([mid, mid, zero], axis=1),
            jnp.concatenate([low, zero, zero], axis=1),
        ]
        parts.append(jnp.concatenate(rows, axis=0))
    total = None
    for c, b in zip(parts, blocks):
        p = bdot(c, b)
        p = p[:R] + (p[R : 2 * R] + p[2 * R :])
        total = p if total is None else total + p
    return total


def pack(v):
    return jnp.concatenate([v[0:8], v[8:16], v[16:24], v[24:32]], axis=1)


def unpack(v):
    return jnp.concatenate([v[:, 0:32], v[:, 32:64], v[:, 64:96], v[:, 96:128]], axis=0)


def factor(gram):
    row = lax.broadcasted_iota(jnp.int32, (R, R), 0)
    col = lax.broadcasted_iota(jnp.int32, (R, R), 1)
    eye = (row == col).astype(F32)
    rid = lax.broadcasted_iota(jnp.int32, (R, 1), 0)
    m = jnp.concatenate([gram, eye], axis=1)
    for k in range(R - 1):
        pivot = m[k : k + 1, :]
        inverse = 1.0 / m[k : k + 1, k : k + 1]
        scale = jnp.where(rid > k, m[:, k : k + 1] * inverse, 0.0)
        m = m - scale * pivot
    upper = m[:, :R]
    diag = jnp.sum(jnp.where(row == col, upper, 0.0), axis=1, keepdims=True)
    rs = 1.0 / jnp.sqrt(diag)
    lower = jnp.where(row <= col, upper * rs, 0.0).T
    return lower, jnp.where(row >= col, m[:, R:] * rs, 0.0)


def permuted(c):
    return jnp.where(c < NCL, ((c >> 3) & 3) * 32 + (c >> 5) * 8 + (c & 7), c)


PER = 66


def num_p(p, h, o):
    return p * PER + h * 3 + o - 1


def num_q(p, h, oa, j):
    return p * PER + 6 + h * 12 + (oa - 1) * 4 + j


def num_z(p, h, s):
    return p * PER + 30 + h * 2 + s


def num_ov(p, h):
    return p * PER + 34 + h


def num_r(p, h, oa, j):
    return p * PER + 36 + h * 12 + (oa - 1) * 4 + j


def num_v(p, h, o):
    return p * PER + 60 + h * 3 + o - 1


QUP = 2 * PER
QDN = QUP + 1
SEM_AR1 = QDN + 1
SEM_AR2 = SEM_AR1 + ND
SEM_FAR1 = SEM_AR2 + NG
SEM_FAR2 = SEM_FAR1 + ND
NSEM = SEM_FAR2 + NG


def kernel(
    rows, cols, scl, table, live, prev, last,
    start_hbm, lbasis_hbm, ltrans_hbm, dtrans_hbm, dcoup_hbm, gcoup_hbm, blocks_hbm,
    next_ref, hess_ref,
    blocks, segc, segr0, segr1, w00, w01, w10, w11, t00, t01, t10, t11, over, ybuf, sbuf, vbuf, mbuf, gbuf, ar1, ar2,
    start, lbasis, ltrans, dtrans, dcoup, gcoup, ltcat, cah, cal, cbh, cbl, dah, dal, dbh, dbl, b1s, b2s, u, bsem, ssem, rsem,
):
    g = lax.axis_index("grp")
    d = lax.axis_index("dev")
    x, y = d // 4, d % 4
    segr = (segr0, segr1)
    w = ((w00, w01), (w10, w11))
    t = ((t00, t01), (t10, t11))
    ab = ((x, y), (y, x))

    def dev(h, a, b):
        return a * 4 + b if h == 0 else b * 4 + a

    def step(v, k):
        return (v + k) % 4

    pairs = (
        (start_hbm, start), (blocks_hbm, blocks), (dcoup_hbm, dcoup), (gcoup_hbm, gcoup),
        (ltrans_hbm, ltrans), (lbasis_hbm, lbasis), (dtrans_hbm, dtrans),
    )
    loads = [pltpu.make_async_copy(src, dst, bsem.at[i]) for i, (src, dst) in enumerate(pairs)]
    for i in (0, 2, 3, 4, 5, 6):
        loads[i].start()

    def remote(src, dst, number, gg, dd):
        return pltpu.make_async_remote_copy(
            src_ref=src, dst_ref=dst, send_sem=ssem.at[number], recv_sem=rsem.at[number],
            device_id=(gg, dd), device_id_type=MESH,
        )

    mbuf[...] = jnp.zeros_like(mbuf)
    gbuf[...] = jnp.zeros_like(gbuf)
    over[...] = jnp.zeros_like(over)
    for p in range(2):
        for h in range(2):
            w[p][h][NCL:WIN] = jnp.zeros((16, RB, HALF), BF16)
        segr[p][NB] = jnp.zeros((R, HALF), F32)
    segc[NB] = jnp.zeros((R, 2 * HALF), F32)

    barrier = pltpu.get_barrier_semaphore()

    def greet_dev(o, c):
        pl.semaphore_signal(barrier, inc=1, device_id=(g, (d + o) % ND), device_id_type=MESH)
        return c

    def greet_grp(o, c):
        pl.semaphore_signal(barrier, inc=1, device_id=((g + o) % NG, d), device_id_type=MESH)
        return c

    lax.fori_loop(1, ND, greet_dev, 0)
    lax.fori_loop(1, NG, greet_grp, 0)

    def all_reduce(i, parts, beside=None, first=False):
        n = 8 * len(parts)
        val = jnp.concatenate([pack(p) for p in parts], axis=0) if len(parts) > 1 else pack(parts[0])
        ar1[i, d, 0:n] = val
        if first:
            pl.semaphore_wait(barrier, ND + NG - 2)

        def along_dev(o):
            return remote(ar1.at[i, d, pl.ds(0, n)], ar1.at[i, d, pl.ds(0, n)], SEM_AR1 + o, g, (d + o) % ND)

        def along_grp(o):
            return remote(ar2.at[i, g, pl.ds(0, n)], ar2.at[i, g, pl.ds(0, n)], SEM_AR2 + o, (g + o) % NG, d)

        def go(make, count):
            lax.fori_loop(1, count, lambda o, c: (make(o).start(), c)[1], 0)

        def got(make, count):
            lax.fori_loop(1, count, lambda o, c: (make(o).wait_recv(), c)[1], 0)

        def left(make, count):
            lax.fori_loop(1, count, lambda o, c: (make(o).wait_send(), c)[1], 0)

        go(along_dev, ND)
        if beside is not None:
            beside()
        got(along_dev, ND)
        total = ar1[i, 0, 0:n]
        for e in range(1, ND):
            total = total + ar1[i, e, 0:n]
        ar2[i, g, 0:n] = total
        go(along_grp, NG)
        left(along_dev, ND)
        got(along_grp, NG)
        total = ar2[i, 0, 0:n]
        for e in range(1, NG):
            total = total + ar2[i, e, 0:n]
        left(along_grp, NG)
        total = total * (1.0 / NPAN)
        return [unpack(total[8 * j : 8 * j + 8]) for j in range(len(parts))]

    def tables():
        loads[1].start()
        for i in range(2, 7):
            loads[i].wait()
        for i in range(CL // 2):
            ltcat[:, 128 * i : 128 * i + 128] = jnp.concatenate([ltrans[2 * i], ltrans[2 * i + 1]], axis=1)

        def build(src, count, ah, al, bh, bl):
            for i in range(count // 2):
                at = slice(128 * i, 128 * i + 128)
                ahead = jnp.concatenate([src[2 * i], src[2 * i + 1]], axis=1)
                ah[:, at], al[:, at] = split(ahead)
                o = count - 1 - 2 * i
                behind = jnp.concatenate([src[o], src[o - 1]], axis=0).T
                bh[:, at], bl[:, at] = split(behind)

        build(dcoup, NOFF, cah, cal, cbh, cbl)
        build(gcoup, GOFF, dah, dal, dbh, dbl)

    def far_send(i):
        return remote(
            mbuf.at[pl.ds((32 + d) * K, K)], mbuf.at[pl.ds((32 + d) * K, K)], SEM_FAR1 + i, g, (d + i) % ND
        )

    def top_send(i):
        return remote(gbuf.at[pl.ds((8 + g) * K, K)], gbuf.at[pl.ds((8 + g) * K, K)], SEM_FAR2 + i, (g + i) % NG, d)

    def shard(p, h, a, b):
        return w[p][h].at[pl.ds((a * 4 + b) * CL, CL)]

    def first(h, s):
        return (0, s) if h == 0 else (s, 0)

    def send_p(p, h, o):
        a, b = ab[h]
        return remote(shard(p, h, a, b), shard(p, h, a, b), num_p(p, h, o), g, dev(h, a, step(b, o)))

    def send_q(p, h, oa, j):
        a, b = ab[h]
        ref = shard(p, h, a, step(b, j))
        return remote(ref, ref, num_q(p, h, oa, j), g, dev(h, step(a, oa), b))

    def send_z(p, h, s):
        a, b = first(h, s)
        return remote(
            shard(p, h, a, b), w[p][h].at[pl.ds(NCL + s * CL, CL)], num_z(p, h, s), (g + NG - 1) % NG, d
        )

    def send_ov(p, h):
        return remote(t[p][h].at[pl.ds(NCL, 16)], over.at[p, h], num_ov(p, h), (g + 1) % NG, d)

    def send_r(p, h, oa, j):
        a, b = ab[h]
        src = t[p][h].at[pl.ds((step(a, oa) * 4 + step(b, j)) * CL, CL)]
        return remote(src, ybuf.at[p, h, oa - 1, j], num_r(p, h, oa, j), g, dev(h, step(a, oa), b))

    def send_v(p, h, o):
        a, b = ab[h]
        return remote(sbuf.at[p, h, o], vbuf.at[p, h, o - 1], num_v(p, h, o), g, dev(h, a, step(b, o)))

    def apply(v, first_call=False):
        vb = v.astype(BF16)
        for p in range(2):
            for h in range(2):
                for c in range(CL):
                    lo = c * 256 + p * HALF
                    w[p][h][(ab[h][0] * 4 + ab[h][1]) * CL + c] = vb[h * RB : h * RB + RB, lo : lo + HALF]

        def along_b(p):
            for o in (1, 3, 2):
                for h in range(2):
                    send_p(p, h, o).start()

        def own_along_a(p):
            for oa in (1, 3, 2):
                for h in range(2):
                    send_q(p, h, oa, 0).start()

        def along_a(p):
            for c in range(4):
                for h in range(2):
                    b = ab[h][1]

                    @pl.when(b != c)
                    def _():
                        send_p(p, h, step(b, 4 - c)).wait_recv()
                        for oa in (1, 3, 2):
                            send_q(p, h, oa, step(c + 4 - b, 0)).start()

        def pass_on(p):
            for h in range(2):
                for s in range(2):
                    sa, sb = first(h, s)
                    a, b = ab[h]

                    @pl.when(a != sa)
                    def _():
                        send_q(p, h, step(a, 4 - sa), step(sb + 4 - b, 0)).wait_recv()

                    @pl.when(g > 0)
                    def _():
                        send_z(p, h, s).start()

        def gathered(p):
            for h in range(2):
                a, b = ab[h]
                for oa in (1, 3, 2):
                    for j in range(4):
                        from_a, from_b = step(a, 4 - oa), step(b, j)
                        if h == 0:
                            early = (from_a == 0) & (from_b < 2)
                        else:
                            early = (from_b == 0) & (from_a < 2)

                        @pl.when(jnp.logical_not(early))
                        def _():
                            send_q(p, h, oa, j).wait_recv()

            @pl.when(g < NG - 1)
            def _():
                for h in range(2):
                    for s in range(2):
                        send_z(p, h, s).wait_recv()

        n_live = live[0]

        def panels(p, c):
            return jnp.concatenate([w[p][0][c], w[p][1][permuted(c)]], axis=0)

        def loop(one):
            def some(i, carry):
                for j in range(UNROLL):
                    k = i * UNROLL + j
                    one(k, jnp.where(k < n_live, table[scl[k]], 0.0))
                return carry

            lax.fori_loop(0, NB // UNROLL, some, 0)

        def near_first(k, weight):
            segc[k] = bdot(panels(0, rows[k]), blocks[k, 0:HALF])

        def near_second(k, weight):
            to_col = segc[k] + bdot(panels(1, rows[k]), blocks[k, HALF : 2 * HALF])
            segc[k] = segc[prev[1, k]] + weight * to_col
            near_row(0, k, weight)

        def near_row(p, k, weight):
            c = cols[k]
            both = jnp.concatenate([panels(0, c), panels(1, c)], axis=1)
            to_row = bdot(blocks[k, p * HALF : p * HALF + HALF], both, NT).T
            segr[p][k] = segr[p][prev[0, k]] + weight * to_row

        def near_total(p, c):
            return segr[p][last[0, c]] + segc[last[1, c], :, p * HALF : p * HALF + HALF]

        def emit(p, i, extra):
            place = ((i // 4, i % 4), (i % 4, i // 4))
            vals = [near_total(p, i * CL + c) for c in range(CL)]
            for h in range(2):
                a, b = ab[h]
                oa, j = step(place[h][0] + 4 - a, 0), step(place[h][1] + 4 - b, 0)
                at = (place[h][0] * 4 + place[h][1]) * CL
                parts = [v[h * RB : h * RB + RB] for v in vals]
                if extra:
                    parts = [v + over[p, h, i * CL + c].astype(F32) for c, v in enumerate(parts)]

                @pl.when(oa == 0)
                def _():
                    for c in range(CL):
                        sbuf[p, h, j, c] = parts[c]

                @pl.when(oa != 0)
                def _():
                    for c in range(CL):
                        t[p][h][at + c] = parts[c].astype(BF16)
                    send_r(p, h, oa, j).start()

        def overflow(p):
            for c in range(NCL, WIN):
                v = near_total(p, c)
                t[p][0][c] = v[:RB].astype(BF16)
                t[p][1][c] = v[RB:].astype(BF16)

            @pl.when(g < NG - 1)
            def _():
                for h in range(2):
                    send_ov(p, h).start()

        def totals(p):
            def one(dx, dy):
                i = step(x, dx) * 4 + step(y, dy)

                @pl.when(i >= 2)
                def _():
                    emit(p, i, False)

                return 0

            lax.fori_loop(0, 9, lambda r, c: one(1 + r // 3, 1 + r % 3), 0)
            lax.fori_loop(1, 4, lambda r, c: one(r, 0), 0)
            lax.fori_loop(0, 4, lambda r, c: one(0, r), 0)

        def first_shards(p):
            @pl.when(g > 0)
            def _():
                for h in range(2):
                    send_ov(p, h).wait_recv()

            for i in range(2):
                emit(p, i, True)

        def summed(p):
            for o in (1, 3, 2, 0):
                for h in range(2):
                    for oa in (1, 3, 2):
                        send_r(p, h, oa, o).wait_recv()
                    sbuf[p, h, o] = sbuf[p, h, o] + (
                        ybuf[p, h, 0, o].astype(F32) + ybuf[p, h, 1, o].astype(F32) + ybuf[p, h, 2, o].astype(F32)
                    )
                    if o:
                        send_v(p, h, o).start()

        along_b(0)
        own_along_a(0)
        along_b(1)
        own_along_a(1)

        q = jnp.concatenate([bdot(lbasis[c], vb[:, 256 * c : 256 * c + 256], NT) for c in range(CL)], axis=0)
        coeffs = dot(ltcat[...], q)
        parents = dot(dtrans[0], coeffs)
        qh, ql = split(coeffs)
        ph, pe = split(parents)
        mbuf[pl.ds(pl.multiple_of((32 + d) * K, K), K), :] = jnp.concatenate([qh, ql, ph, pe], axis=1)

        along_a(0)
        pass_on(0)
        along_a(1)
        gathered(0)
        if first_call:
            loads[1].wait()
        loop(near_first)
        pass_on(1)
        gathered(1)
        lax.fori_loop(1, ND, lambda o, c: (far_send(o).start(), c)[1], 0)
        loop(near_second)
        overflow(0)
        totals(0)
        loop(lambda k, weight: near_row(1, k, weight))
        overflow(1)
        totals(1)
        first_shards(0)

        lax.fori_loop(1, ND, lambda o, c: (far_send(o).wait_recv(), c)[1], 0)
        group_rows = pl.ds(32 * K, ND * K)
        up = remote(mbuf.at[group_rows], mbuf.at[pl.ds(16 * K, ND * K)], QUP, (g + 1) % NG, d)
        down = remote(mbuf.at[group_rows], mbuf.at[pl.ds(48 * K, ND * K)], QDN, (g + NG - 1) % NG, d)

        @pl.when(g < NG - 1)
        def _():
            up.start()

        @pl.when(g > 0)
        def _():
            down.start()

        top = mbuf[32 * K : 33 * K, :].astype(F32)
        for e in range(1, ND):
            top = top + mbuf[(32 + e) * K : (33 + e) * K, :].astype(F32)
        gh, gl = split(top[:, 64:96] + top[:, 96:128])
        gbuf[pl.ds(pl.multiple_of((8 + g) * K, K), K), :] = jnp.concatenate(
            [gh, gl, jnp.zeros((K, 64), BF16)], axis=1
        )
        lax.fori_loop(1, NG, lambda o, c: (top_send(o).start(), c)[1], 0)

        first_shards(1)
        summed(0)
        summed(1)

        lax.fori_loop(1, NG, lambda o, c: (top_send(o).wait_recv(), c)[1], 0)

        @pl.when(g > 0)
        def _():
            up.wait_recv()

        @pl.when(g < NG - 1)
        def _():
            down.wait_recv()

        ga = gbuf[pl.ds(pl.multiple_of((10 + g) * K, K), GOFF * K), :]
        gb = gbuf[pl.ds(pl.multiple_of((1 + g) * K, K), GOFF * K), :]
        s1 = bdot(dah[...], ga) + bdot(dbh[...], gb)
        s2 = bdot(dal[...], ga) + bdot(dbl[...], gb)
        top_field = s1[:, 0:32] + s1[:, 32:64] + s2[:, 0:32]
        qa = mbuf[pl.ds(pl.multiple_of((34 + d) * K, K), NOFF * K), :]
        qb = mbuf[pl.ds(pl.multiple_of((1 + d) * K, K), NOFF * K), :]
        s1 = bdot(cah[...], qa) + bdot(cbh[...], qb)
        s2 = bdot(cal[...], qa) + bdot(cbl[...], qb)
        field = s1[:, 0:32] + s1[:, 32:64] + s2[:, 0:32]
        field_t = field.T + dot(top_field.T, dtrans[0])
        leaf_t = dot(field_t, ltcat[...])
        lh, ll = split(leaf_t)
        for c in range(CL):
            both = jnp.concatenate([lh[:, K * c : K * c + K], ll[:, K * c : K * c + K]], axis=0)
            far = bdot(both, lbasis[c])
            u[:, 256 * c : 256 * c + 256] = far[:R] + far[R:]

        lax.fori_loop(1, ND, lambda o, c: (far_send(o).wait_send(), c)[1], 0)
        lax.fori_loop(1, NG, lambda o, c: (top_send(o).wait_send(), c)[1], 0)
        @pl.when(g < NG - 1)
        def _():
            up.wait_send()

        @pl.when(g > 0)
        def _():
            down.wait_send()

        for p in range(2):
            for h in range(2):
                for o in (1, 3, 2):
                    send_v(p, h, o).wait_recv()
                for c in range(CL):
                    total = sbuf[p, h, 0, c] + vbuf[p, h, 0, c] + vbuf[p, h, 1, c] + vbuf[p, h, 2, c]
                    at = (slice(h * RB, h * RB + RB), slice(256 * c + p * HALF, 256 * c + p * HALF + HALF))
                    u[at] = u[at] + total

        for p in range(2):
            for h in range(2):
                for o in range(1, 4):
                    send_p(p, h, o).wait_send()
                    send_v(p, h, o).wait_send()
                    for j in range(4):
                        send_q(p, h, o, j).wait_send()
                        send_r(p, h, o, j).wait_send()

                @pl.when(g > 0)
                def _():
                    for s in range(2):
                        send_z(p, h, s).wait_send()

                @pl.when(g < NG - 1)
                def _():
                    send_ov(p, h).wait_send()

    row = lax.broadcasted_iota(jnp.int32, (R, R), 0)
    col = lax.broadcasted_iota(jnp.int32, (R, R), 1)
    half_eye = jnp.where(row == col, 0.5, 0.0)

    tn = (((0,), (0,)), ((), ()))
    loads[0].wait()
    ss = terms(start[...])
    (gram,) = all_reduce(0, [inner(ss, ss)], beside=tables, first=True)
    _, inverse = factor(gram)
    v = combine([inverse], [ss])
    b1s[...] = terms(v)
    apply(v, first_call=True)

    us = terms(u[...])
    ha, gram = all_reduce(1, [inner(b1s[...], us), inner(us, us)])
    lower1, inverse = factor(gram - dot(ha, ha, tn))
    v = combine([inverse, -dot(inverse, ha, NT)], [us, b1s[...]])
    b2s[...] = terms(v)
    hess_ref[0] = ha + half_eye
    hess_ref[1] = lower1
    apply(v)

    us = terms(u[...])
    hb, hc, gram = all_reduce(2, [inner(b1s[...], us), inner(b2s[...], us), inner(us, us)])
    lower2, inverse = factor(gram - dot(hb, hb, tn) - dot(hc, hc, tn))
    next_ref[...] = combine(
        [inverse, -dot(inverse, hb, NT), -dot(inverse, hc, NT)], [us, b1s[...], b2s[...]]
    )
    hess_ref[2] = hb
    hess_ref[3] = hc + half_eye
    hess_ref[4] = lower2


def chains(near_rows, near_cols):
    target = jnp.stack([near_rows, near_cols])
    order = jnp.arange(NB, dtype=jnp.int32)
    before = (target[:, :, None] == target[:, None, :]) & (order[None, :] < order[:, None])[None]
    prev = jnp.max(jnp.where(before, order, -1), axis=2)
    hit = jnp.arange(WIN, dtype=jnp.int32)[None, :, None] == target[:, None, :]
    last = jnp.max(jnp.where(hit, order, -1), axis=2)
    return jnp.where(prev < 0, NB, prev), jnp.where(last < 0, NB, last)


def shards(
    start, near_blocks, near_rows, near_cols, near_scale, scale_table, near_live,
    leaf_basis, leaf_transfer, device_transfer, device_coupling, group_coupling,
):
    prev, last = chains(near_rows, near_cols)
    smem = pl.BlockSpec(memory_space=pltpu.SMEM)
    vmem = pl.BlockSpec(memory_space=pltpu.VMEM)
    anywhere = pl.BlockSpec(memory_space=pltpu.HBM)
    outs = (jax.ShapeDtypeStruct((R, 2048), F32), jax.ShapeDtypeStruct((5, R, R), F32))
    return pl.pallas_call(
        kernel,
        out_shape=outs,
        in_specs=[smem] * 7 + [anywhere] * 7,
        out_specs=(vmem, vmem),
        scratch_shapes=[
            pltpu.VMEM((NB, 256, 256), BF16),
            pltpu.VMEM((NB + 1, R, 256), F32),
            pltpu.VMEM((NB + 1, R, HALF), F32),
            pltpu.VMEM((NB + 1, R, HALF), F32),
            pltpu.VMEM((WIN, RB, HALF), BF16),
            pltpu.VMEM((WIN, RB, HALF), BF16),
            pltpu.VMEM((WIN, RB, HALF), BF16),
            pltpu.VMEM((WIN, RB, HALF), BF16),
            pltpu.VMEM((WIN, RB, HALF), BF16),
            pltpu.VMEM((WIN, RB, HALF), BF16),
            pltpu.VMEM((WIN, RB, HALF), BF16),
            pltpu.VMEM((WIN, RB, HALF), BF16),
            pltpu.VMEM((2, 2, 16, RB, HALF), BF16),
            pltpu.VMEM((2, 2, 3, 4, CL, RB, HALF), BF16),
            pltpu.VMEM((2, 2, 4, CL, RB, HALF), F32),
            pltpu.VMEM((2, 2, 3, CL, RB, HALF), F32),
            pltpu.VMEM((80 * K, 128), BF16),
            pltpu.VMEM((24 * K, 128), BF16),
            pltpu.VMEM((3, ND, 24, 128), F32),
            pltpu.VMEM((3, NG, 24, 128), F32),
            pltpu.VMEM((R, 2048), F32),
            pltpu.VMEM((CL, K, 256), BF16),
            pltpu.VMEM((CL, K, K), F32),
            pltpu.VMEM((1, K, K), F32),
            pltpu.VMEM((NOFF, K, K), F32),
            pltpu.VMEM((GOFF, K, K), F32),
            pltpu.VMEM((K, CL * K), F32),
            pltpu.VMEM((K, NOFF * K), BF16),
            pltpu.VMEM((K, NOFF * K), BF16),
            pltpu.VMEM((K, NOFF * K), BF16),
            pltpu.VMEM((K, NOFF * K), BF16),
            pltpu.VMEM((K, GOFF * K), BF16),
            pltpu.VMEM((K, GOFF * K), BF16),
            pltpu.VMEM((K, GOFF * K), BF16),
            pltpu.VMEM((K, GOFF * K), BF16),
            pltpu.VMEM((3 * R, 2048), BF16),
            pltpu.VMEM((3 * R, 2048), BF16),
            pltpu.VMEM((R, 2048), F32),
            pltpu.SemaphoreType.DMA((7,)),
            pltpu.SemaphoreType.DMA((NSEM,)),
            pltpu.SemaphoreType.DMA((NSEM,)),
        ],
        compiler_params=pltpu.CompilerParams(
            collective_id=0, has_side_effects=True, vmem_limit_bytes=60 * 2**20
        ),
        name="arnoldi",
    )(
        near_rows, near_cols, near_scale, scale_table, near_live, prev, last,
        start, leaf_basis, leaf_transfer, device_transfer, device_coupling, group_coupling, near_blocks,
    )


def solution(mesh):
    both = ("grp", "dev")
    cut = P(both, None, None)
    return jax.shard_map(
        shards,
        mesh=mesh,
        in_specs=(P(None, both), cut, P(both), P(both), P(both), P(), P(both), cut, cut, cut, P(), P()),
        out_specs=(P(None, both), P()),
        check_vma=False,
    )
```
